32 devices in a mesh: img: 4 (over y, core), ref: 8 (over z, x).
Axes of the slice: x: 2, y: 2, z: 4, core: 2. Of those that a mesh axis runs over, the one named last changes fastest.
Arguments:
- images: float32 [2, 64, 32768], P(None, 'img', 'ref'), may hold values from -6 to 6
- references: float32 [2, 64, 32768], P(None, 'ref', 'img'), may hold values from -2 to 2
- precision: float32 [64], P('img'), may hold values from 0.00390625 to 0.0390625
- shifts: int32 [12, 2], replicated, may hold values from -6 to 6, as said below
- labels: int32 [64], P('ref'), may hold values from 0 to 3
- log_prior: float32 [4], replicated, may hold values from -4 to 4
Outputs:
- new_refs: float32 [2, 64, 32768], P(None, 'ref', 'img')
- class_post: float32 [64, 4], P('img')
The draws below stay inside these ranges and needn't reach their ends.
Inputs may be any that keep to these rules, and one draw needn't show every extreme that they name: `shifts`: both ends of the range occur in every draw.
All inputs are finite; a program needn't handle non-finite values.
Results may differ from the reference program's by a relative error of at most 0.0056.
Values may be sent and summed in bfloat16 or wider, within the bound.
A program may use at most 64 MiB of HBM per device.

```python
import math
import jax
import jax.numpy as jnp
from jax import lax

ROWS = 256
COLS = 128
SHIFTS = 12
CLASSES = 4
IMAGES = 64
REFS = 64


def shift_table(key):
    base = jax.random.fold_in(key, 202)
    first, second, third = jax.random.split(base, 3)
    table = jax.random.randint(first, (SHIFTS, 2), -6, 7, dtype=jnp.int32)
    low_row = jax.random.randint(second, (), 0, SHIFTS, dtype=jnp.int32)
    high_row = jax.random.randint(third, (), 0, SHIFTS, dtype=jnp.int32)
    row_index = jnp.arange(SHIFTS, dtype=jnp.int32)[:, None]
    col_index = jnp.arange(2, dtype=jnp.int32)[None, :]
    table = jnp.where((row_index == low_row) & (col_index == 0), jnp.int32(-6), table)
    table = jnp.where((row_index == high_row) & (col_index == 1), jnp.int32(6), table)
    return table.astype(jnp.int32)


def ref_table(key):
    base = jax.random.fold_in(key, 101)
    first, second = jax.random.split(base, 2)
    phase = jax.random.uniform(first, (REFS, ROWS * COLS), jnp.float32, -math.pi, math.pi)
    level = jax.random.uniform(second, (REFS, ROWS * COLS), jnp.float32, 0.85, 1.05)
    profile = jnp.ones((1, ROWS * COLS), jnp.float32)
    amplitude = jnp.sqrt(2.0 * profile) * level
    return jnp.stack([amplitude * jnp.cos(phase), amplitude * jnp.sin(phase)]).astype(jnp.float32)


def bright_plan(key):
    base = jax.random.fold_in(key, 404)
    first, second, third, fourth = jax.random.split(base, 4)
    marks = jax.random.randint(first, (IMAGES,), 0, 8, dtype=jnp.int32)
    forced = jax.random.randint(second, (), 0, IMAGES, dtype=jnp.int32)
    bright = (marks == 0) | (jnp.arange(IMAGES, dtype=jnp.int32) == forced)
    strength = jax.random.uniform(third, (IMAGES,), jnp.float32, 150.0, 300.0)
    offset = jax.random.randint(fourth, (IMAGES,), 1, REFS, dtype=jnp.int32)
    return (bright, strength, offset)


def draw_shifts(key, part):
    return shift_table(key)


def draw_references(key, part):
    return ref_table(key)


def draw_precision(key, part):
    bright, strength, offset = bright_plan(key)
    base = jax.random.fold_in(key, 505)
    lo = 1.0 / (2.0 * ROWS * COLS) ** 0.5
    hi = 10.0 / (2.0 * ROWS * COLS) ** 0.5
    drawn = jnp.exp(jax.random.uniform(base, (IMAGES,), jnp.float32, math.log(lo), math.log(hi)))
    return jnp.where(bright, strength / (ROWS * COLS), drawn).astype(jnp.float32)


def draw_images(key, part):
    refs = ref_table(key)
    table = shift_table(key)
    bright, strength, offset = bright_plan(key)
    base = jax.random.fold_in(key, 303)
    first, second, third, fourth, fifth = jax.random.split(base, 5)
    chosen = jax.random.randint(first, (IMAGES,), 0, REFS, dtype=jnp.int32)
    partner = (chosen + offset) % REFS
    which = jax.random.randint(second, (IMAGES,), 0, SHIFTS, dtype=jnp.int32)
    index = jnp.arange(ROWS * COLS, dtype=jnp.int32)
    freq_y = (index // COLS - ROWS // 2).astype(jnp.float32)
    freq_x = (index % COLS).astype(jnp.float32)
    shift_x = table[which, 0].astype(jnp.float32)[:, None]
    shift_y = table[which, 1].astype(jnp.float32)[:, None]
    angles = 2.0 * math.pi / ROWS * (freq_x[None, :] * shift_x + freq_y[None, :] * shift_y)
    cosine = jnp.cos(angles)
    sine_part = jnp.sin(angles)
    picked = refs[:, chosen, :]
    other = refs[:, partner, :]
    signal = jnp.stack([picked[0] * cosine + picked[1] * sine_part, picked[1] * cosine - picked[0] * sine_part])
    second_signal = jnp.stack([other[0] * cosine + other[1] * sine_part, other[1] * cosine - other[0] * sine_part])
    signal_weight = jnp.exp(jax.random.uniform(fourth, (IMAGES,), jnp.float32, 0.0, math.log(48.0)))
    signal_weight = signal_weight / (2.0 * ROWS * COLS) ** 0.5
    noise_level = jax.random.uniform(fifth, (IMAGES,), jnp.float32, 0.75, 1.2)
    noise = jax.random.truncated_normal(third, -4.5, 4.5, (2, IMAGES, ROWS * COLS), jnp.float32)
    drawn = signal_weight[None, :, None] * signal + noise_level[None, :, None] * noise
    mixed = signal + (1.0 - 1.0 / strength)[None, :, None] * second_signal + 0.02 * noise
    result = jnp.where(bright[None, :, None], mixed, drawn)
    return jnp.clip(result, -6.0, 6.0).astype(jnp.float32)


def place_ends(entries, key, least, top_value):
    place = [jax.random.randint(jax.random.fold_in(key, axis), (), 0, length) for axis, length in enumerate(entries.shape)]
    widest = entries.shape.index(max(entries.shape))
    neighbour = place[:widest] + [(place[widest] + 1) % entries.shape[widest]] + place[widest + 1:]
    return entries.at[tuple(place)].set(least).at[tuple(neighbour)].set(top_value)


def normal_values(stream_key, shape, width, most, held_as=jnp.bfloat16):
    return jnp.clip(width * jax.random.normal(stream_key, shape, jnp.float32), -most, most).astype(held_as)


def setup_inputs(seed: int = 0) -> dict:
    keys = jax.random.split(jax.random.key(seed), 7)
    images = draw_images(jax.random.fold_in(keys[6], 71), 0)
    references = draw_references(jax.random.fold_in(keys[6], 71), 0)
    precision = draw_precision(jax.random.fold_in(keys[6], 71), 0)
    shifts = draw_shifts(jax.random.fold_in(keys[6], 71), 0)
    labels = place_ends(jax.random.randint(keys[4], (REFS,), 0, CLASSES), jax.random.fold_in(keys[4], 1), 0, CLASSES - 1).astype(jnp.int32)
    log_prior = normal_values(keys[5], (CLASSES,), 1.0, 4.0, jnp.float32)
    return {"images": images, "references": references, "precision": precision, "shifts": shifts, "labels": labels, "log_prior": log_prior}


def phases(shifts):
    index = jnp.arange(ROWS * COLS, dtype=jnp.int32)
    freq_y = (index // COLS - ROWS // 2).astype(jnp.float32)
    freq_x = (index % COLS).astype(jnp.float32)
    shift_x = shifts[:, 0].astype(jnp.float32)[:, None]
    shift_y = shifts[:, 1].astype(jnp.float32)[:, None]
    angles = (2.0 * math.pi / ROWS) * (freq_x[None, :] * shift_x + freq_y[None, :] * shift_y)
    return jnp.cos(angles), jnp.sin(angles)


def reference(images, references, precision, shifts, labels, log_prior):
    img_low = images.astype(jnp.bfloat16)
    ref_low = references.astype(jnp.bfloat16)
    cosine, sine_part = phases(shifts)
    ref_wide = ref_low.astype(jnp.float32)
    energy = jnp.sum(ref_wide * ref_wide, axis=(0, 2))
    onehot = (labels[:, None] == jnp.arange(CLASSES, dtype=jnp.int32)[None, :]).astype(jnp.float32)
    prior_term = jnp.sum(onehot * log_prior[None, :], axis=1)

    def cross_one(operands):
        cos_row, sin_row = operands
        shifted_re = (ref_wide[0] * cos_row[None, :] + ref_wide[1] * sin_row[None, :]).astype(jnp.bfloat16)
        shifted_im = (ref_wide[1] * cos_row[None, :] - ref_wide[0] * sin_row[None, :]).astype(jnp.bfloat16)
        return (jnp.dot(img_low[0], shifted_re.T, preferred_element_type=jnp.float32)
                + jnp.dot(img_low[1], shifted_im.T, preferred_element_type=jnp.float32))

    cross_terms = lax.map(cross_one, (cosine, sine_part))
    scores = precision[None, :, None] * (cross_terms - 0.5 * energy[None, None, :]) + prior_term[None, None, :]
    top_score = jnp.max(scores, axis=(0, 2))
    exponent = jnp.exp(scores - top_score[None, :, None])
    row_total = jnp.sum(exponent, axis=(0, 2))
    posterior = exponent / row_total[None, :, None]
    class_post = jnp.einsum("ik,kc->ic", jnp.sum(posterior, axis=0), onehot, precision=lax.Precision.HIGHEST)
    ref_mass = jnp.sum(posterior, axis=(0, 1))
    post_low = posterior.astype(jnp.bfloat16)

    def back_one(running, operands):
        weights_row, cos_row, sin_row = operands
        back_re = jnp.dot(weights_row.T, img_low[0], preferred_element_type=jnp.float32)
        back_im = jnp.dot(weights_row.T, img_low[1], preferred_element_type=jnp.float32)
        update = jnp.stack([back_re * cos_row[None, :] - back_im * sin_row[None, :],
                            back_im * cos_row[None, :] + back_re * sin_row[None, :]])
        return running + update, None

    start_sum = jnp.zeros((2, labels.shape[0], ROWS * COLS), jnp.float32)
    summed, unused = lax.scan(back_one, start_sum, (post_low, cosine, sine_part))
    new_refs = summed / (ref_mass + 1.0)[None, :, None]
    return new_refs, class_post
```

```python
import functools
import math

import jax
import jax.numpy as jnp
from jax import lax
from jax.experimental import pallas as pl
from jax.experimental.pallas import tpu as pltpu
from jax.sharding import PartitionSpec as P

ROWS = 256
COLS = 128
SHIFTS = 12
CLASSES = 4


def phases(shifts):
    index = jnp.arange(ROWS * COLS, dtype=jnp.int32)
    freq_y = (index // COLS - ROWS // 2).astype(jnp.float32)
    freq_x = (index % COLS).astype(jnp.float32)
    shift_x = shifts[:, 0].astype(jnp.float32)[:, None]
    shift_y = shifts[:, 1].astype(jnp.float32)[:, None]
    angles = 2.0 * math.pi / ROWS * (freq_x[None, :] * shift_x + freq_y[None, :] * shift_y)
    return (jnp.cos(angles), jnp.sin(angles))


def inner_rows(left, right):
    return lax.dot_general(
        left, right, (((1,), (1,)), ((), ())), preferred_element_type=jnp.float32
    )


def inner_cols(left, right):
    return lax.dot_general(
        left, right, (((0,), (0,)), ((), ())), preferred_element_type=jnp.float32
    )


def gathered(images, references, precision, shifts, labels, log_prior):
    img_low = lax.all_gather(images.astype(jnp.bfloat16), "ref", axis=2, tiled=True)
    ref_low = lax.all_gather(references.astype(jnp.bfloat16), "img", axis=2, tiled=True)
    pixels = img_low.shape[2]
    img_dev = img_low.shape[1]
    ref_dev = ref_low.shape[1]
    blocks = SHIFTS // 4
    cosine, sine_part = phases(shifts)
    cos_blocks = cosine.reshape(blocks, 4, pixels)
    sin_blocks = sine_part.reshape(blocks, 4, pixels)
    ref_wide = ref_low.astype(jnp.float32)
    energy = jnp.sum(ref_wide * ref_wide, axis=(0, 2))
    onehot = (labels[:, None] == jnp.arange(CLASSES, dtype=jnp.int32)[None, :]).astype(jnp.float32)
    prior_term = jnp.sum(onehot * log_prior[None, :], axis=1)

    def cross_block(operands):
        cos_rows, sin_rows = operands
        shifted_re = (
            ref_wide[0][None] * cos_rows[:, None, :] + ref_wide[1][None] * sin_rows[:, None, :]
        ).astype(jnp.bfloat16)
        shifted_im = (
            ref_wide[1][None] * cos_rows[:, None, :] - ref_wide[0][None] * sin_rows[:, None, :]
        ).astype(jnp.bfloat16)
        return inner_rows(img_low[0], shifted_re.reshape(4 * ref_dev, pixels)) + inner_rows(
            img_low[1], shifted_im.reshape(4 * ref_dev, pixels)
        )

    cross_terms = lax.map(cross_block, (cos_blocks, sin_blocks))
    cross_terms = jnp.transpose(cross_terms, (1, 0, 2)).reshape(img_dev, SHIFTS, ref_dev)
    scores = (
        precision[:, None, None] * (cross_terms - 0.5 * energy[None, None, :])
        + prior_term[None, None, :]
    )
    local_top = jnp.max(scores, axis=(1, 2))
    top_score = lax.pmax(local_top, "ref")
    exponent = jnp.exp(scores - top_score[:, None, None])
    local_class = jnp.einsum(
        "ik,kc->ic", jnp.sum(exponent, axis=1), onehot, precision=lax.Precision.HIGHEST
    )
    row_total, class_sum = lax.psum((jnp.sum(exponent, axis=(1, 2)), local_class), "ref")
    posterior = exponent / row_total[:, None, None]
    class_post = class_sum / row_total[:, None]
    local_mass = jnp.sum(posterior, axis=(0, 1))
    post_low = posterior.astype(jnp.bfloat16).reshape(img_dev, blocks, 4 * ref_dev)
    post_low = jnp.transpose(post_low, (1, 0, 2))

    def back_block(running, operands):
        weights_blk, cos_rows, sin_rows = operands
        back_re = inner_cols(weights_blk, img_low[0]).reshape(4, ref_dev, pixels)
        back_im = inner_cols(weights_blk, img_low[1]).reshape(4, ref_dev, pixels)
        part_re = jnp.sum(back_re * cos_rows[:, None, :] - back_im * sin_rows[:, None, :], axis=0)
        part_im = jnp.sum(back_im * cos_rows[:, None, :] + back_re * sin_rows[:, None, :], axis=0)
        return (running + jnp.stack([part_re, part_im]), None)

    start_sum = jnp.zeros((2, ref_dev, pixels), jnp.float32)
    summed, unused = lax.scan(back_block, start_sum, (post_low, cos_blocks, sin_blocks))
    summed_part = lax.psum_scatter(summed, "img", scatter_dimension=2, tiled=True)
    ref_mass = lax.psum(local_mass, "img")
    new_refs = summed_part / (ref_mass + 1.0)[None, :, None]
    return (new_refs, class_post)


MESH = pl.DeviceIdType.MESH
LANES = 128
CHUNK = 1024
OWNED = 2
PAIRS = SHIFTS // 2
REF_ROWS = 8


def exchange(src, dst, send_sem, recv_sem, img, ref):
    return pltpu.make_async_remote_copy(
        src_ref=src, dst_ref=dst, send_sem=send_sem, recv_sem=recv_sem, device_id=(img, ref), device_id_type=MESH
    )


def fused_kernel(
    n_img, n_ref,
    images, references, precision, shifts, labels, log_prior,
    new_refs, class_post,
    img_send, img_buf, ref_send, ref_buf, cos_tab, sin_tab, rotated, shifted,
    part, part_in, own, own_in, post_buf, post_wide, out_send, out_buf,
    img_ss, img_rs, ref_ss, ref_rs, part_ss, part_rs, own_ss, own_rs, post_ss, post_rs, out_ss, out_rs,
):
    n_dev = n_img * n_ref
    a = lax.axis_index("img")
    r = lax.axis_index("ref")
    me = a * n_ref + r
    per = n_ref // n_img
    img_dev = images.shape[1]
    n_images = n_img * img_dev
    n_refs = n_ref * REF_ROWS

    barrier = pltpu.get_barrier_semaphore()

    def greet(j, carry):
        other = lax.rem(me + j, n_dev)
        pl.semaphore_signal(barrier, inc=1, device_id=(other // n_ref, lax.rem(other, n_ref)), device_id_type=MESH)
        return carry

    lax.fori_loop(1, n_dev, greet, 0)

    for q in range(n_ref):
        px = pl.ds(q * CHUNK, CHUNK)
        both = jnp.concatenate([references[0, :, px], references[1, :, px]], axis=0)
        ref_send[q, :, 0:CHUNK] = both.astype(jnp.bfloat16)
    label_col = jnp.broadcast_to(labels[...].astype(jnp.float32), (REF_ROWS, LANES))
    label_block = jnp.concatenate([label_col, label_col], axis=0).astype(jnp.bfloat16)
    for q in range(n_ref):
        ref_send[q, :, CHUNK : CHUNK + LANES] = label_block
    for q in range(n_img):
        img_send[q] = images[:, :, q * CHUNK : (q + 1) * CHUNK].astype(jnp.bfloat16)
    img_buf[a] = img_send[a]

    pl.semaphore_wait(barrier, n_dev - 1)

    def ref_copy(q):
        return exchange(
            ref_send.at[q], ref_buf.at[r], ref_ss.at[q], ref_rs.at[r], lax.rem(q, n_img), per * a + q // n_img
        )

    def ref_here(q):
        return (lax.rem(q, n_img) == a) & (per * a + q // n_img == r)

    def ref_start(j, carry):
        q = lax.rem(me + j, n_ref)

        @pl.when(ref_here(q))
        def _():
            ref_buf[r] = ref_send[q]

        @pl.when(jnp.logical_not(ref_here(q)))
        def _():
            ref_copy(q).start()

        return carry

    lax.fori_loop(0, n_ref, ref_start, 0)

    img_copies = []
    for j in range(1, n_img):
        dest = lax.rem(a + j, n_img)
        copy = exchange(img_send.at[dest], img_buf.at[a], img_ss.at[j], img_rs.at[j], dest, r)
        copy.start()
        img_copies.append(copy)

    row_first = r * (n_img * CHUNK // COLS) + a * (CHUNK // COLS) - ROWS // 2
    freq_y = lax.broadcasted_iota(jnp.int32, (CHUNK // COLS, COLS), 0) + row_first
    freq_x = lax.broadcasted_iota(jnp.int32, (CHUNK // COLS, COLS), 1)

    def phase_row(t, carry):
        turn = freq_x * shifts[t, 0] + freq_y * shifts[t, 1]
        turn = ((turn + ROWS // 2) & (ROWS - 1)) - ROWS // 2
        angle = turn.astype(jnp.float32) * (2.0 * math.pi / ROWS)
        cosine = jnp.cos(angle)
        sine = jnp.sin(angle)
        for y in range(CHUNK // COLS):
            cos_tab[t, :, y * COLS : (y + 1) * COLS] = jnp.broadcast_to(cosine[y : y + 1], (8, COLS))
            sin_tab[t, :, y * COLS : (y + 1) * COLS] = jnp.broadcast_to(sine[y : y + 1], (8, COLS))
        return carry

    lax.fori_loop(0, SHIFTS, phase_row, 0)

    for copy in img_copies:
        copy.wait_recv()

    def rotate(t, carry):
        cos_row = cos_tab[t][None]
        sin_row = sin_tab[t][None]
        for b in range(n_img):
            re = img_buf[b, 0].astype(jnp.float32).reshape(img_dev // 8, 8, CHUNK)
            im = img_buf[b, 1].astype(jnp.float32).reshape(img_dev // 8, 8, CHUNK)
            rows = pl.ds(b * img_dev, img_dev)
            turned_re = (re * cos_row - im * sin_row).reshape(img_dev, CHUNK)
            turned_im = (im * cos_row + re * sin_row).reshape(img_dev, CHUNK)
            rotated[t, rows, 0:CHUNK] = turned_re.astype(jnp.bfloat16)
            rotated[t, rows, CHUNK : 2 * CHUNK] = turned_im.astype(jnp.bfloat16)
        return carry

    lax.fori_loop(0, SHIFTS, rotate, 0)

    def ref_arrive(j, carry):
        @pl.when(jnp.logical_not((a == r // per) & (j == r)))
        def _():
            exchange(ref_send.at[0], ref_buf.at[j], ref_ss.at[0], ref_rs.at[j], r // per, j).wait_recv()

        return carry

    lax.fori_loop(0, n_ref, ref_arrive, 0)

    def shift(t, carry):
        cos_row = cos_tab[t]
        sin_row = sin_tab[t]
        for b in range(0, n_ref, 2):
            res = []
            ims = []
            for s in range(2):
                block = ref_buf[b + s, :, 0:CHUNK].astype(jnp.float32)
                re = block[0:REF_ROWS]
                im = block[REF_ROWS : 2 * REF_ROWS]
                res.append(re * cos_row + im * sin_row)
                ims.append(im * cos_row - re * sin_row)
            rows = pl.ds(b * REF_ROWS, 2 * REF_ROWS)
            shifted[t, rows, 0:CHUNK] = jnp.concatenate(res, axis=0).astype(jnp.bfloat16)
            shifted[t, rows, CHUNK : 2 * CHUNK] = jnp.concatenate(ims, axis=0).astype(jnp.bfloat16)
        return carry

    lax.fori_loop(0, SHIFTS, shift, 0)

    energies = []
    label_rows = []
    for b in range(n_ref):
        block = ref_buf[b, :, 0:CHUNK].astype(jnp.float32)
        square = jnp.sum(block * block, axis=1, keepdims=True)
        energies.append(square[0:REF_ROWS] + square[REF_ROWS : 2 * REF_ROWS])
        label_rows.append(ref_buf[b, :, CHUNK : CHUNK + LANES].astype(jnp.float32)[0:REF_ROWS])
    energy = jnp.broadcast_to(jnp.concatenate(energies + energies, axis=0), (2 * n_refs, LANES)).T
    half_energy = 0.5 * energy[0:8][None]
    label_lane = jnp.concatenate(label_rows + label_rows, axis=0).T[0:8]

    pictures = [img_buf[:, c].reshape(n_images, CHUNK) for c in range(2)]
    pictures = jnp.concatenate(pictures, axis=1)
    for tp in range(PAIRS):
        pair = shifted[2 * tp : 2 * tp + 2].reshape(2 * n_refs, 2 * CHUNK)
        cross = inner_rows(pictures, pair)
        cross = (cross.reshape(n_images // 8, 8, LANES) - half_energy).reshape(n_img, img_dev, LANES)
        part[:, :, tp * LANES : (tp + 1) * LANES] = cross

    part_copies = []
    for j in range(1, n_img):
        dest = lax.rem(a + j, n_img)
        copy = exchange(part.at[dest], part_in.at[j - 1], part_ss.at[j], part_rs.at[j], dest, r)
        copy.start()
        part_copies.append(copy)
    own[...] = jnp.zeros_like(own)
    for copy in part_copies:
        copy.wait_recv()
    total = part[a]
    for j in range(n_img - 1):
        total = total + part_in[j]
    for tp in range(PAIRS):
        own[:, tp, :] = total[:, tp * LANES : (tp + 1) * LANES]
    own_copies = []
    for j in range(1, n_ref):
        dest = lax.rem(r + j, n_ref)
        copy = exchange(own.at[pl.ds(OWNED * dest, OWNED)], own_in.at[j - 1], own_ss.at[j], own_rs.at[j], a, dest)
        copy.start()
        own_copies.append(copy)
    prior = jnp.zeros((8, LANES), jnp.float32)
    for c in range(CLASSES):
        prior = prior + jnp.where(label_lane == c, log_prior[c], 0.0)
    for copy in own_copies:
        copy.wait_recv()
    mine = own[pl.ds(OWNED * r, OWNED)]
    for j in range(n_ref - 1):
        mine = mine + own_in[j]

    row = lax.broadcasted_iota(jnp.int32, (8, LANES), 0)
    lane = lax.broadcasted_iota(jnp.int32, (8, LANES), 1)
    blocks = []
    for il in range(OWNED):
        scores = precision[OWNED * r + il] * mine[il] + prior
        scores = jnp.where(row < PAIRS, scores, -jnp.inf)
        top = jnp.max(jnp.max(scores, axis=1, keepdims=True), axis=0, keepdims=True)
        exponent = jnp.exp(scores - top)
        row_total = jnp.sum(jnp.sum(exponent, axis=1, keepdims=True), axis=0, keepdims=True)
        posterior = exponent / row_total
        lane_sum = jnp.broadcast_to(jnp.sum(posterior, axis=0, keepdims=True), (8, LANES))
        totals = lane_sum + pltpu.roll(lane_sum, n_refs, 1)
        for c in range(CLASSES):
            in_class = jnp.sum(jnp.where(label_lane == c, lane_sum, 0.0), axis=1, keepdims=True)
            totals = jnp.where(lane == n_refs + c, in_class, totals)
        high = totals.astype(jnp.bfloat16).astype(jnp.float32)
        block = jnp.where(row == PAIRS, high, posterior)
        blocks.append(jnp.where(row == PAIRS + 1, totals - high, block))
    post_buf[me] = jnp.concatenate(blocks, axis=0).astype(jnp.bfloat16)

    def post_copy(j):
        other = lax.rem(me + j, n_dev)
        return exchange(
            post_buf.at[me], post_buf.at[me], post_ss.at[j], post_rs.at[j], other // n_ref, lax.rem(other, n_ref)
        )

    def post_start(j, carry):
        post_copy(j).start()
        return carry

    lax.fori_loop(1, n_dev, post_start, 0)

    def post_arrive(j, carry):
        source = lax.rem(me + n_dev - j, n_dev)
        exchange(
            post_buf.at[me], post_buf.at[source], post_ss.at[j], post_rs.at[j], source // n_ref, lax.rem(source, n_ref)
        ).wait_recv()
        return carry

    lax.fori_loop(1, n_dev, post_arrive, 0)

    post_wide[...] = post_buf[...].astype(jnp.float32).reshape(n_images, 8, LANES)
    totals = post_wide[:, PAIRS, :] + post_wide[:, PAIRS + 1, :]
    mass = jnp.broadcast_to(jnp.sum(totals, axis=0, keepdims=True), (LANES, LANES)).T[0:n_refs]
    scale = 1.0 / (mass[:, 0:1] + 1.0)
    first = pl.ds(a * img_dev, img_dev)
    class_post[...] = post_wide[first, PAIRS, :] + post_wide[first, PAIRS + 1, :]
    weights = []
    for tp in range(PAIRS):
        both = post_wide[:, tp, :].T
        weights.append(jnp.concatenate([both[0:n_refs], both[n_refs : 2 * n_refs]], axis=1).astype(jnp.bfloat16))
    weights = jnp.concatenate(weights, axis=1)
    turned = rotated[...].reshape(SHIFTS * n_images, 2 * CHUNK)
    summed = jnp.dot(weights, turned, preferred_element_type=jnp.float32) * scale
    low = summed.reshape(n_ref, REF_ROWS, 2 * CHUNK)
    for b in range(n_ref):
        both = jnp.concatenate([low[b, :, 0:CHUNK], low[b, :, CHUNK : 2 * CHUNK]], axis=0)
        out_send[b] = both.astype(jnp.bfloat16)

    piece = lax.rem(r, per) * n_img + a

    def out_copy(j):
        return exchange(out_send.at[j], out_buf.at[piece], out_ss.at[j], out_rs.at[piece], r // per, j)

    def out_start(i, carry):
        j = lax.rem(r + i, n_ref)
        here = (a == r // per) & (j == r)

        @pl.when(here)
        def _():
            out_buf[piece] = out_send[j]

        @pl.when(jnp.logical_not(here))
        def _():
            out_copy(j).start()

        return carry

    lax.fori_loop(0, n_ref, out_start, 0)

    for q in range(n_ref):
        @pl.when(jnp.logical_not(ref_here(q)))
        def _():
            exchange(
                out_send.at[0], out_buf.at[q], out_ss.at[0], out_rs.at[q], q % n_img, per * a + q // n_img
            ).wait_recv()

        block = out_buf[q].astype(jnp.float32)
        new_refs[0, :, q * CHUNK : (q + 1) * CHUNK] = block[0:REF_ROWS]
        new_refs[1, :, q * CHUNK : (q + 1) * CHUNK] = block[REF_ROWS : 2 * REF_ROWS]

    for copy in img_copies + part_copies + own_copies:
        copy.wait_send()

    def post_sent(j, carry):
        post_copy(j).wait_send()
        return carry

    lax.fori_loop(1, n_dev, post_sent, 0)

    def edge_sent(j, carry):
        @pl.when(jnp.logical_not(ref_here(j)))
        def _():
            ref_copy(j).wait_send()

        @pl.when(jnp.logical_not((a == r // per) & (j == r)))
        def _():
            out_copy(j).wait_send()

        return carry

    lax.fori_loop(0, n_ref, edge_sent, 0)


def fused(n_img, n_ref, images, references, precision, shifts, labels, log_prior):
    img_dev = images.shape[1]
    n_images = n_img * img_dev
    n_refs = n_ref * REF_ROWS
    n_dev = n_img * n_ref
    vmem = pl.BlockSpec(memory_space=pltpu.VMEM)
    smem = pl.BlockSpec(memory_space=pltpu.SMEM)
    low = jnp.bfloat16
    wide = jnp.float32
    counts = (n_img, n_img, n_ref, n_ref, n_img, n_img, n_ref, n_ref, n_dev, n_dev, n_ref, n_ref)
    new_refs, class_rows = pl.pallas_call(
        functools.partial(fused_kernel, n_img, n_ref),
        out_shape=(
            jax.ShapeDtypeStruct(references.shape, wide),
            jax.ShapeDtypeStruct((img_dev, LANES), wide),
        ),
        in_specs=[vmem, vmem, smem, smem, vmem, smem],
        out_specs=(vmem, vmem),
        scratch_shapes=[
            pltpu.VMEM((n_img, 2, img_dev, CHUNK), low),
            pltpu.VMEM((n_img, 2, img_dev, CHUNK), low),
            pltpu.VMEM((n_ref, 2 * REF_ROWS, CHUNK + LANES), low),
            pltpu.VMEM((n_ref, 2 * REF_ROWS, CHUNK + LANES), low),
            pltpu.VMEM((SHIFTS, 8, CHUNK), wide),
            pltpu.VMEM((SHIFTS, 8, CHUNK), wide),
            pltpu.VMEM((SHIFTS, n_images, 2 * CHUNK), low),
            pltpu.VMEM((SHIFTS, n_refs, 2 * CHUNK), low),
            pltpu.VMEM((n_img, img_dev, PAIRS * LANES), wide),
            pltpu.VMEM((n_img - 1, img_dev, PAIRS * LANES), wide),
            pltpu.VMEM((img_dev, 8, LANES), wide),
            pltpu.VMEM((n_ref - 1, OWNED, 8, LANES), wide),
            pltpu.VMEM((n_dev, 16, LANES), low),
            pltpu.VMEM((n_images, 8, LANES), wide),
            pltpu.VMEM((n_ref, 2 * REF_ROWS, CHUNK), low),
            pltpu.VMEM((n_ref, 2 * REF_ROWS, CHUNK), low),
        ]
        + [pltpu.SemaphoreType.DMA((count,)) for count in counts],
        compiler_params=pltpu.CompilerParams(
            collective_id=0, has_side_effects=True, vmem_limit_bytes=40 * 1024 * 1024
        ),
        cost_estimate=pl.CostEstimate(flops=800_000_000, bytes_accessed=2_000_000, transcendentals=25_000),
    )(images, references, precision, shifts, labels.reshape(REF_ROWS, 1), log_prior)
    return new_refs, class_rows[:, n_refs : n_refs + CLASSES]


def local(n_img, n_ref, images, references, precision, shifts, labels, log_prior):
    fits = (
        images.shape[1] == OWNED * n_ref
        and images.shape[1] % 16 == 0
        and references.shape[1] == REF_ROWS
        and 2 * n_ref * REF_ROWS == LANES
        and images.shape[2] == n_img * CHUNK
        and references.shape[2] == n_ref * CHUNK
        and n_ref % n_img == 0
    )
    if fits:
        return fused(n_img, n_ref, images, references, precision, shifts, labels, log_prior)
    return gathered(images, references, precision, shifts, labels, log_prior)


def solution(mesh):
    return jax.shard_map(
        functools.partial(local, mesh.shape["img"], mesh.shape["ref"]),
        mesh=mesh,
        in_specs=(P(None, "img", "ref"), P(None, "ref", "img"), P("img"), P(), P("ref"), P()),
        out_specs=(P(None, "ref", "img"), P("img", None)),
        check_vma=False,
    )
```

```python
import functools
import math

import jax
import jax.numpy as jnp
from jax import lax
from jax.experimental import pallas as pl
from jax.experimental.pallas import tpu as pltpu
from jax.sharding import PartitionSpec as P

ROWS = 256
COLS = 128
SHIFTS = 12
CLASSES = 4


def phases(shifts):
    index = jnp.arange(ROWS * COLS, dtype=jnp.int32)
    freq_y = (index // COLS - ROWS // 2).astype(jnp.float32)
    freq_x = (index % COLS).astype(jnp.float32)
    shift_x = shifts[:, 0].astype(jnp.float32)[:, None]
    shift_y = shifts[:, 1].astype(jnp.float32)[:, None]
    angles = 2.0 * math.pi / ROWS * (freq_x[None, :] * shift_x + freq_y[None, :] * shift_y)
    return (jnp.cos(angles), jnp.sin(angles))


def inner_rows(left, right):
    return lax.dot_general(
        left, right, (((1,), (1,)), ((), ())), preferred_element_type=jnp.float32
    )


def inner_cols(left, right):
    return lax.dot_general(
        left, right, (((0,), (0,)), ((), ())), preferred_element_type=jnp.float32
    )


def gathered(images, references, precision, shifts, labels, log_prior):
    img_low = lax.all_gather(images.astype(jnp.bfloat16), "ref", axis=2, tiled=True)
    ref_low = lax.all_gather(references.astype(jnp.bfloat16), "img", axis=2, tiled=True)
    pixels = img_low.shape[2]
    img_dev = img_low.shape[1]
    ref_dev = ref_low.shape[1]
    blocks = SHIFTS // 4
    cosine, sine_part = phases(shifts)
    cos_blocks = cosine.reshape(blocks, 4, pixels)
    sin_blocks = sine_part.reshape(blocks, 4, pixels)
    ref_wide = ref_low.astype(jnp.float32)
    energy = jnp.sum(ref_wide * ref_wide, axis=(0, 2))
    onehot = (labels[:, None] == jnp.arange(CLASSES, dtype=jnp.int32)[None, :]).astype(jnp.float32)
    prior_term = jnp.sum(onehot * log_prior[None, :], axis=1)

    def cross_block(operands):
        cos_rows, sin_rows = operands
        shifted_re = (
            ref_wide[0][None] * cos_rows[:, None, :] + ref_wide[1][None] * sin_rows[:, None, :]
        ).astype(jnp.bfloat16)
        shifted_im = (
            ref_wide[1][None] * cos_rows[:, None, :] - ref_wide[0][None] * sin_rows[:, None, :]
        ).astype(jnp.bfloat16)
        return inner_rows(img_low[0], shifted_re.reshape(4 * ref_dev, pixels)) + inner_rows(
            img_low[1], shifted_im.reshape(4 * ref_dev, pixels)
        )

    cross_terms = lax.map(cross_block, (cos_blocks, sin_blocks))
    cross_terms = jnp.transpose(cross_terms, (1, 0, 2)).reshape(img_dev, SHIFTS, ref_dev)
    scores = (
        precision[:, None, None] * (cross_terms - 0.5 * energy[None, None, :])
        + prior_term[None, None, :]
    )
    local_top = jnp.max(scores, axis=(1, 2))
    top_score = lax.pmax(local_top, "ref")
    exponent = jnp.exp(scores - top_score[:, None, None])
    local_class = jnp.einsum(
        "ik,kc->ic", jnp.sum(exponent, axis=1), onehot, precision=lax.Precision.HIGHEST
    )
    row_total, class_sum = lax.psum((jnp.sum(exponent, axis=(1, 2)), local_class), "ref")
    posterior = exponent / row_total[:, None, None]
    class_post = class_sum / row_total[:, None]
    local_mass = jnp.sum(posterior, axis=(0, 1))
    post_low = posterior.astype(jnp.bfloat16).reshape(img_dev, blocks, 4 * ref_dev)
    post_low = jnp.transpose(post_low, (1, 0, 2))

    def back_block(running, operands):
        weights_blk, cos_rows, sin_rows = operands
        back_re = inner_cols(weights_blk, img_low[0]).reshape(4, ref_dev, pixels)
        back_im = inner_cols(weights_blk, img_low[1]).reshape(4, ref_dev, pixels)
        part_re = jnp.sum(back_re * cos_rows[:, None, :] - back_im * sin_rows[:, None, :], axis=0)
        part_im = jnp.sum(back_im * cos_rows[:, None, :] + back_re * sin_rows[:, None, :], axis=0)
        return (running + jnp.stack([part_re, part_im]), None)

    start_sum = jnp.zeros((2, ref_dev, pixels), jnp.float32)
    summed, unused = lax.scan(back_block, start_sum, (post_low, cos_blocks, sin_blocks))
    summed_part = lax.psum_scatter(summed, "img", scatter_dimension=2, tiled=True)
    ref_mass = lax.psum(local_mass, "img")
    new_refs = summed_part / (ref_mass + 1.0)[None, :, None]
    return (new_refs, class_post)


MESH = pl.DeviceIdType.MESH
LANES = 128
CHUNK = 1024
OWNED = 2
PAIRS = SHIFTS // 2
TOGETHER = 4
GROUPS = SHIFTS // TOGETHER
STRIP = 512
REF_ROWS = 8


def exchange(src, dst, send_sem, recv_sem, img, ref):
    return pltpu.make_async_remote_copy(
        src_ref=src, dst_ref=dst, send_sem=send_sem, recv_sem=recv_sem, device_id=(img, ref), device_id_type=MESH
    )


def fused_kernel(
    n_img, n_ref,
    images_hbm, references_hbm, precision_hbm, shifts_hbm, labels_hbm, log_prior_hbm,
    new_refs, class_post,
    images, references, precision, shifts, labels, log_prior,
    img_send, img_buf, ref_send, ref_buf, cos_tab, sin_tab, rotated, shifted,
    energy_col, part, part_in, own, own_in, post_buf, post_wide, out_send, out_buf, in_sem,
    img_ss, img_rs, ref_ss, ref_rs, part_ss, part_rs, own_ss, own_rs, post_ss, post_rs, out_ss, out_rs,
):
    n_dev = n_img * n_ref
    a = lax.axis_index("img")
    r = lax.axis_index("ref")
    me = a * n_ref + r
    per = n_ref // n_img
    img_dev = images.shape[1]
    n_images = n_img * img_dev
    n_refs = n_ref * REF_ROWS

    loads = [
        pltpu.make_async_copy(src, dst, in_sem.at[i])
        for i, (src, dst) in enumerate(
            (
                (references_hbm, references),
                (images_hbm, images),
                (shifts_hbm, shifts),
                (precision_hbm, precision),
                (labels_hbm, labels),
                (log_prior_hbm, log_prior),
            )
        )
    ]
    for load in loads:
        load.start()

    barrier = pltpu.get_barrier_semaphore()

    def greet(j, carry):
        other = lax.rem(me + j, n_dev)
        pl.semaphore_signal(barrier, inc=1, device_id=(other // n_ref, lax.rem(other, n_ref)), device_id_type=MESH)
        return carry

    lax.fori_loop(1, n_dev, greet, 0)

    loads[0].wait()
    for q in range(n_ref):
        px = pl.ds(q * CHUNK, CHUNK)
        both = jnp.concatenate([references[0, :, px], references[1, :, px]], axis=0)
        ref_send[q] = both.astype(jnp.bfloat16)

    pl.semaphore_wait(barrier, n_dev - 1)

    def ref_copy(q):
        return exchange(
            ref_send.at[q], ref_buf.at[r], ref_ss.at[q], ref_rs.at[r], lax.rem(q, n_img), per * a + q // n_img
        )

    def ref_here(q):
        return (lax.rem(q, n_img) == a) & (per * a + q // n_img == r)

    def ref_start(j, carry):
        q = lax.rem(me + j, n_ref)

        @pl.when(ref_here(q))
        def _():
            ref_buf[r] = ref_send[q]

        @pl.when(jnp.logical_not(ref_here(q)))
        def _():
            ref_copy(q).start()

        return carry

    lax.fori_loop(0, n_ref, ref_start, 0)

    loads[1].wait()
    for q in range(n_img):
        img_send[q] = images[:, :, q * CHUNK : (q + 1) * CHUNK].astype(jnp.bfloat16)
    img_buf[a] = img_send[a]
    img_copies = []
    for j in range(1, n_img):
        dest = lax.rem(a + j, n_img)
        copy = exchange(img_send.at[dest], img_buf.at[a], img_ss.at[j], img_rs.at[j], dest, r)
        copy.start()
        img_copies.append(copy)

    row_first = r * (n_img * CHUNK // COLS) + a * (CHUNK // COLS) - ROWS // 2
    freq_y = lax.broadcasted_iota(jnp.int32, (CHUNK // COLS, COLS), 0) + row_first
    freq_x = lax.broadcasted_iota(jnp.int32, (CHUNK // COLS, COLS), 1)

    for load in loads[2:]:
        load.wait()
    for t in range(SHIFTS):
        turn = freq_x * shifts[0:1, t : t + 1] + freq_y * shifts[1:2, t : t + 1]
        turn = ((turn + ROWS // 2) & (ROWS - 1)) - ROWS // 2
        angle = turn.astype(jnp.float32) * (2.0 * math.pi / ROWS)
        cosine = jnp.cos(angle)
        sine = jnp.sin(angle)
        for y in range(CHUNK // COLS):
            cos_tab[t, :, y * COLS : (y + 1) * COLS] = jnp.broadcast_to(cosine[y : y + 1], (8, COLS))
            sin_tab[t, :, y * COLS : (y + 1) * COLS] = jnp.broadcast_to(sine[y : y + 1], (8, COLS))

    row = lax.broadcasted_iota(jnp.int32, (8, LANES), 0)
    lane = lax.broadcasted_iota(jnp.int32, (8, LANES), 1)
    label_row = jnp.concatenate([labels[...].astype(jnp.float32)] * (LANES // REF_ROWS), axis=1)
    label_row = jnp.where((lane // REF_ROWS) % n_ref == r, jnp.broadcast_to(label_row, (8, LANES)), 0.0)

    for copy in img_copies:
        copy.wait_recv()

    def rotate(t, carry):
        cos_row = cos_tab[t][None]
        sin_row = sin_tab[t][None]
        for b in range(n_img):
            re = img_buf[b, 0].astype(jnp.float32).reshape(img_dev // 8, 8, CHUNK)
            im = img_buf[b, 1].astype(jnp.float32).reshape(img_dev // 8, 8, CHUNK)
            rows = pl.ds(b * img_dev, img_dev)
            turned_re = (re * cos_row - im * sin_row).reshape(img_dev, CHUNK)
            turned_im = (im * cos_row + re * sin_row).reshape(img_dev, CHUNK)
            rotated[t, rows, 0:CHUNK] = turned_re.astype(jnp.bfloat16)
            rotated[t, rows, CHUNK : 2 * CHUNK] = turned_im.astype(jnp.bfloat16)
        return carry

    lax.fori_loop(0, SHIFTS, rotate, 0)

    def arrive(b):
        @pl.when(jnp.logical_not((a == r // per) & (b == r)))
        def _():
            exchange(ref_send.at[0], ref_buf.at[b], ref_ss.at[0], ref_rs.at[b], r // per, b).wait_recv()

    def shift(b, t):
        cos_row = cos_tab[t]
        sin_row = sin_tab[t]
        res = []
        ims = []
        for s in range(2):
            block = ref_buf[b + s].astype(jnp.float32)
            re = block[0:REF_ROWS]
            im = block[REF_ROWS : 2 * REF_ROWS]
            res.append(re * cos_row + im * sin_row)
            ims.append(im * cos_row - re * sin_row)
        rows = pl.ds(pl.multiple_of(b * REF_ROWS, 2 * REF_ROWS), 2 * REF_ROWS)
        shifted[t, rows, 0:CHUNK] = jnp.concatenate(res, axis=0).astype(jnp.bfloat16)
        shifted[t, rows, CHUNK : 2 * CHUNK] = jnp.concatenate(ims, axis=0).astype(jnp.bfloat16)

    def ready(b):
        arrive(b)
        arrive(b + 1)
        for s in range(2):
            block = ref_buf[b + s].astype(jnp.float32)
            square = jnp.sum(block * block, axis=1, keepdims=True)
            square = jnp.broadcast_to(square[0:REF_ROWS] + square[REF_ROWS : 2 * REF_ROWS], (REF_ROWS, LANES))
            energy_col[pl.ds(pl.multiple_of((b + s) * REF_ROWS, REF_ROWS), REF_ROWS)] = square

    layers = n_ref // 2

    def layer_step(i, carry):
        b = 2 * lax.rem(r // 2 + i, layers)
        ready(b)

        def turn_step(t, inner):
            shift(b, t)
            return inner

        return lax.fori_loop(0, SHIFTS, turn_step, carry)

    lax.fori_loop(0, layers - 1, layer_step, 0)
    last = 2 * lax.rem(r // 2 + layers - 1, layers)
    ready(last)
    energy = energy_col[...]
    half_energy = 0.5 * jnp.concatenate([energy, energy], axis=0).T[0:8][None]

    pictures = [img_buf[:, c].reshape(n_images, CHUNK) for c in range(2)]
    pictures = jnp.concatenate(pictures, axis=1)
    part_copies = []
    for g in range(GROUPS):
        for t in range(g * TOGETHER, (g + 1) * TOGETHER):
            shift(last, t)
        group = shifted[g * TOGETHER : (g + 1) * TOGETHER].reshape(TOGETHER * n_refs, 2 * CHUNK)
        cross = inner_rows(pictures, group)
        for h in range(TOGETHER // 2):
            pair = cross[:, h * LANES : (h + 1) * LANES]
            pair = (pair.reshape(n_images // 8, 8, LANES) - half_energy).reshape(n_img, img_dev, LANES)
            part[g, :, :, h * LANES : (h + 1) * LANES] = pair
        for j in range(1, n_img):
            dest = lax.rem(a + j, n_img)
            copy = exchange(
                part.at[g, dest], part_in.at[g, j - 1], part_ss.at[g, j], part_rs.at[g, j], dest, r
            )
            copy.start()
            part_copies.append(copy)

    own[...] = jnp.zeros_like(own)
    own[:, PAIRS, :] = jnp.broadcast_to(label_row[0:1], (img_dev, LANES))
    for copy in part_copies:
        copy.wait_recv()
    for g in range(GROUPS):
        total = part[g, a]
        for j in range(n_img - 1):
            total = total + part_in[g, j]
        for h in range(TOGETHER // 2):
            own[:, g * (TOGETHER // 2) + h, :] = total[:, h * LANES : (h + 1) * LANES]
    own_copies = []
    for j in range(1, n_ref):
        dest = lax.rem(r + j, n_ref)
        copy = exchange(own.at[pl.ds(OWNED * dest, OWNED)], own_in.at[j - 1], own_ss.at[j], own_rs.at[j], a, dest)
        copy.start()
        own_copies.append(copy)
    for copy in own_copies:
        copy.wait_recv()
    mine = own[pl.ds(OWNED * r, OWNED)]
    for j in range(n_ref - 1):
        mine = mine + own_in[j]
    label_lane = jnp.broadcast_to(mine[0, PAIRS : PAIRS + 1], (8, LANES))
    prior = jnp.zeros((8, LANES), jnp.float32)
    for c in range(CLASSES):
        prior = prior + jnp.where(label_lane == c, log_prior[:, c : c + 1], 0.0)
    image_lane = lax.broadcasted_iota(jnp.int32, (1, img_dev), 1)

    blocks = []
    for il in range(OWNED):
        noise = jnp.sum(jnp.where(image_lane == OWNED * r + il, precision[...], 0.0), axis=1, keepdims=True)
        scores = noise * mine[il] + prior
        scores = jnp.where(row < PAIRS, scores, -jnp.inf)
        top = jnp.max(jnp.max(scores, axis=1, keepdims=True), axis=0, keepdims=True)
        exponent = jnp.exp(scores - top)
        row_total = jnp.sum(jnp.sum(exponent, axis=1, keepdims=True), axis=0, keepdims=True)
        posterior = exponent / row_total
        lane_sum = jnp.broadcast_to(jnp.sum(posterior, axis=0, keepdims=True), (8, LANES))
        totals = lane_sum + pltpu.roll(lane_sum, n_refs, 1)
        for c in range(CLASSES):
            in_class = jnp.sum(jnp.where(label_lane == c, lane_sum, 0.0), axis=1, keepdims=True)
            totals = jnp.where(lane == n_refs + c, in_class, totals)
        high = totals.astype(jnp.bfloat16).astype(jnp.float32)
        block = jnp.where(row == PAIRS, high, posterior)
        blocks.append(jnp.where(row == PAIRS + 1, totals - high, block))
    post_buf[me] = jnp.concatenate(blocks, axis=0).astype(jnp.bfloat16)

    def post_copy(j):
        other = lax.rem(me + j, n_dev)
        return exchange(
            post_buf.at[me], post_buf.at[me], post_ss.at[j], post_rs.at[j], other // n_ref, lax.rem(other, n_ref)
        )

    def post_start(j, carry):
        post_copy(j).start()
        return carry

    lax.fori_loop(1, n_dev, post_start, 0)

    def post_arrive(j, carry):
        source = lax.rem(me + n_dev - j, n_dev)
        exchange(
            post_buf.at[me], post_buf.at[source], post_ss.at[j], post_rs.at[j], source // n_ref, lax.rem(source, n_ref)
        ).wait_recv()
        return carry

    lax.fori_loop(1, n_dev, post_arrive, 0)

    post_wide[...] = post_buf[...].astype(jnp.float32).reshape(n_images, 8, LANES)
    totals = post_wide[:, PAIRS, :] + post_wide[:, PAIRS + 1, :]
    mass = jnp.broadcast_to(jnp.sum(totals, axis=0, keepdims=True), (LANES, LANES)).T[0:n_refs]
    scale = 1.0 / (mass[:, 0:1] + 1.0)
    first = pl.ds(a * img_dev, img_dev)
    mine = post_wide[first, PAIRS, :] + post_wide[first, PAIRS + 1, :]
    class_post[...] = jnp.concatenate([mine] * (LANES // img_dev), axis=0).T[n_refs : n_refs + CLASSES, 0:img_dev]
    weights = []
    for tp in range(PAIRS):
        both = post_wide[:, tp, :].T
        weights.append(jnp.concatenate([both[0:n_refs], both[n_refs : 2 * n_refs]], axis=1).astype(jnp.bfloat16))
    weights = jnp.concatenate(weights, axis=1)
    turned = rotated[...].reshape(SHIFTS * n_images, 2 * CHUNK)
    piece = lax.rem(r, per) * n_img + a

    def out_copy(h, j):
        return exchange(
            out_send.at[h, j], out_buf.at[h, piece], out_ss.at[h, j], out_rs.at[h, piece], r // per, j
        )

    for h in range(CHUNK // STRIP):
        real = jnp.dot(weights, turned[:, h * STRIP : (h + 1) * STRIP], preferred_element_type=jnp.float32)
        imag = jnp.dot(
            weights, turned[:, CHUNK + h * STRIP : CHUNK + (h + 1) * STRIP], preferred_element_type=jnp.float32
        )
        real = (real * scale).reshape(n_ref, REF_ROWS, STRIP)
        imag = (imag * scale).reshape(n_ref, REF_ROWS, STRIP)
        out_send[h] = jnp.concatenate([real, imag], axis=1).astype(jnp.bfloat16)

        def out_start(i, carry):
            j = lax.rem(r + i, n_ref)
            here = (a == r // per) & (j == r)

            @pl.when(here)
            def _():
                out_buf[h, piece] = out_send[h, j]

            @pl.when(jnp.logical_not(here))
            def _():
                out_copy(h, j).start()

            return carry

        lax.fori_loop(0, n_ref, out_start, 0)

    for h in range(CHUNK // STRIP):
        for q in range(n_ref):
            @pl.when(jnp.logical_not(ref_here(q)))
            def _():
                exchange(
                    out_send.at[h, 0], out_buf.at[h, q], out_ss.at[h, 0], out_rs.at[h, q],
                    q % n_img, per * a + q // n_img,
                ).wait_recv()

            block = out_buf[h, q].astype(jnp.float32)
            px = slice(q * CHUNK + h * STRIP, q * CHUNK + (h + 1) * STRIP)
            new_refs[0, :, px] = block[0:REF_ROWS]
            new_refs[1, :, px] = block[REF_ROWS : 2 * REF_ROWS]

    for copy in img_copies + part_copies + own_copies:
        copy.wait_send()

    def post_sent(j, carry):
        post_copy(j).wait_send()
        return carry

    lax.fori_loop(1, n_dev, post_sent, 0)

    def edge_sent(j, carry):
        @pl.when(jnp.logical_not(ref_here(j)))
        def _():
            ref_copy(j).wait_send()

        @pl.when(jnp.logical_not((a == r // per) & (j == r)))
        def _():
            for h in range(CHUNK // STRIP):
                out_copy(h, j).wait_send()

        return carry

    lax.fori_loop(0, n_ref, edge_sent, 0)


def fused(n_img, n_ref, images, references, precision, shifts, labels, log_prior):
    img_dev = images.shape[1]
    n_images = n_img * img_dev
    n_refs = n_ref * REF_ROWS
    n_dev = n_img * n_ref
    vmem = pl.BlockSpec(memory_space=pltpu.VMEM)
    far = pl.BlockSpec(memory_space=pl.ANY)
    low = jnp.bfloat16
    wide = jnp.float32
    strips = CHUNK // STRIP
    parts = (GROUPS, n_img)
    outs = (strips, n_ref)
    counts = ((6,), (n_img,), (n_img,), (n_ref,), (n_ref,), parts, parts)
    counts = counts + ((n_ref,), (n_ref,), (n_dev,), (n_dev,), outs, outs)
    new_refs, class_rows = pl.pallas_call(
        functools.partial(fused_kernel, n_img, n_ref),
        out_shape=(
            jax.ShapeDtypeStruct(references.shape, wide),
            jax.ShapeDtypeStruct((CLASSES, img_dev), wide),
        ),
        in_specs=[far] * 6,
        out_specs=(vmem, vmem),
        scratch_shapes=[
            pltpu.VMEM(images.shape, wide),
            pltpu.VMEM(references.shape, wide),
            pltpu.VMEM((1, img_dev), wide),
            pltpu.VMEM((2, SHIFTS), jnp.int32),
            pltpu.VMEM((1, REF_ROWS), jnp.int32),
            pltpu.VMEM((1, CLASSES), wide),
            pltpu.VMEM((n_img, 2, img_dev, CHUNK), low),
            pltpu.VMEM((n_img, 2, img_dev, CHUNK), low),
            pltpu.VMEM((n_ref, 2 * REF_ROWS, CHUNK), low),
            pltpu.VMEM((n_ref, 2 * REF_ROWS, CHUNK), low),
            pltpu.VMEM((SHIFTS, 8, CHUNK), wide),
            pltpu.VMEM((SHIFTS, 8, CHUNK), wide),
            pltpu.VMEM((SHIFTS, n_images, 2 * CHUNK), low),
            pltpu.VMEM((SHIFTS, n_refs, 2 * CHUNK), low),
            pltpu.VMEM((n_refs, LANES), wide),
            pltpu.VMEM((GROUPS, n_img, img_dev, TOGETHER * n_refs), wide),
            pltpu.VMEM((GROUPS, n_img - 1, img_dev, TOGETHER * n_refs), wide),
            pltpu.VMEM((img_dev, 8, LANES), wide),
            pltpu.VMEM((n_ref - 1, OWNED, 8, LANES), wide),
            pltpu.VMEM((n_dev, 16, LANES), low),
            pltpu.VMEM((n_images, 8, LANES), wide),
            pltpu.VMEM((strips, n_ref, 2 * REF_ROWS, STRIP), low),
            pltpu.VMEM((strips, n_ref, 2 * REF_ROWS, STRIP), low),
        ]
        + [pltpu.SemaphoreType.DMA(count) for count in counts],
        compiler_params=pltpu.CompilerParams(
            collective_id=0, has_side_effects=True, vmem_limit_bytes=56 * 1024 * 1024
        ),
        cost_estimate=pl.CostEstimate(flops=800_000_000, bytes_accessed=2_000_000, transcendentals=25_000),
    )(
        images,
        references,
        precision.reshape(1, img_dev),
        shifts.T,
        labels.reshape(1, REF_ROWS),
        log_prior.reshape(1, CLASSES),
    )
    return new_refs, class_rows.T


def local(n_img, n_ref, images, references, precision, shifts, labels, log_prior):
    fits = (
        images.shape[1] == OWNED * n_ref
        and images.shape[1] % 16 == 0
        and references.shape[1] == REF_ROWS
        and 2 * n_ref * REF_ROWS == LANES
        and images.shape[2] == n_img * CHUNK
        and references.shape[2] == n_ref * CHUNK
        and n_ref % n_img == 0
    )
    if fits:
        return fused(n_img, n_ref, images, references, precision, shifts, labels, log_prior)
    return gathered(images, references, precision, shifts, labels, log_prior)


def solution(mesh):
    return jax.shard_map(
        functools.partial(local, mesh.shape["img"], mesh.shape["ref"]),
        mesh=mesh,
        in_specs=(P(None, "img", "ref"), P(None, "ref", "img"), P("img"), P(), P("ref"), P()),
        out_specs=(P(None, "ref", "img"), P("img", None)),
        check_vma=False,
    )
```

```python
import functools
import math

import jax
import jax.numpy as jnp
from jax import lax
from jax.experimental import pallas as pl
from jax.experimental.pallas import tpu as pltpu
from jax.sharding import PartitionSpec as P

ROWS = 256
COLS = 128
SHIFTS = 12
CLASSES = 4


def phases(shifts):
    index = jnp.arange(ROWS * COLS, dtype=jnp.int32)
    freq_y = (index // COLS - ROWS // 2).astype(jnp.float32)
    freq_x = (index % COLS).astype(jnp.float32)
    shift_x = shifts[:, 0].astype(jnp.float32)[:, None]
    shift_y = shifts[:, 1].astype(jnp.float32)[:, None]
    angles = 2.0 * math.pi / ROWS * (freq_x[None, :] * shift_x + freq_y[None, :] * shift_y)
    return (jnp.cos(angles), jnp.sin(angles))


def inner_rows(left, right):
    return lax.dot_general(
        left, right, (((1,), (1,)), ((), ())), preferred_element_type=jnp.float32
    )


def inner_cols(left, right):
    return lax.dot_general(
        left, right, (((0,), (0,)), ((), ())), preferred_element_type=jnp.float32
    )


def gathered(images, references, precision, shifts, labels, log_prior):
    img_low = lax.all_gather(images.astype(jnp.bfloat16), "ref", axis=2, tiled=True)
    ref_low = lax.all_gather(references.astype(jnp.bfloat16), "img", axis=2, tiled=True)
    pixels = img_low.shape[2]
    img_dev = img_low.shape[1]
    ref_dev = ref_low.shape[1]
    blocks = SHIFTS // 4
    cosine, sine_part = phases(shifts)
    cos_blocks = cosine.reshape(blocks, 4, pixels)
    sin_blocks = sine_part.reshape(blocks, 4, pixels)
    ref_wide = ref_low.astype(jnp.float32)
    energy = jnp.sum(ref_wide * ref_wide, axis=(0, 2))
    onehot = (labels[:, None] == jnp.arange(CLASSES, dtype=jnp.int32)[None, :]).astype(jnp.float32)
    prior_term = jnp.sum(onehot * log_prior[None, :], axis=1)

    def cross_block(operands):
        cos_rows, sin_rows = operands
        shifted_re = (
            ref_wide[0][None] * cos_rows[:, None, :] + ref_wide[1][None] * sin_rows[:, None, :]
        ).astype(jnp.bfloat16)
        shifted_im = (
            ref_wide[1][None] * cos_rows[:, None, :] - ref_wide[0][None] * sin_rows[:, None, :]
        ).astype(jnp.bfloat16)
        return inner_rows(img_low[0], shifted_re.reshape(4 * ref_dev, pixels)) + inner_rows(
            img_low[1], shifted_im.reshape(4 * ref_dev, pixels)
        )

    cross_terms = lax.map(cross_block, (cos_blocks, sin_blocks))
    cross_terms = jnp.transpose(cross_terms, (1, 0, 2)).reshape(img_dev, SHIFTS, ref_dev)
    scores = (
        precision[:, None, None] * (cross_terms - 0.5 * energy[None, None, :])
        + prior_term[None, None, :]
    )
    local_top = jnp.max(scores, axis=(1, 2))
    top_score = lax.pmax(local_top, "ref")
    exponent = jnp.exp(scores - top_score[:, None, None])
    local_class = jnp.einsum(
        "ik,kc->ic", jnp.sum(exponent, axis=1), onehot, precision=lax.Precision.HIGHEST
    )
    row_total, class_sum = lax.psum((jnp.sum(exponent, axis=(1, 2)), local_class), "ref")
    posterior = exponent / row_total[:, None, None]
    class_post = class_sum / row_total[:, None]
    local_mass = jnp.sum(posterior, axis=(0, 1))
    post_low = posterior.astype(jnp.bfloat16).reshape(img_dev, blocks, 4 * ref_dev)
    post_low = jnp.transpose(post_low, (1, 0, 2))

    def back_block(running, operands):
        weights_blk, cos_rows, sin_rows = operands
        back_re = inner_cols(weights_blk, img_low[0]).reshape(4, ref_dev, pixels)
        back_im = inner_cols(weights_blk, img_low[1]).reshape(4, ref_dev, pixels)
        part_re = jnp.sum(back_re * cos_rows[:, None, :] - back_im * sin_rows[:, None, :], axis=0)
        part_im = jnp.sum(back_im * cos_rows[:, None, :] + back_re * sin_rows[:, None, :], axis=0)
        return (running + jnp.stack([part_re, part_im]), None)

    start_sum = jnp.zeros((2, ref_dev, pixels), jnp.float32)
    summed, unused = lax.scan(back_block, start_sum, (post_low, cos_blocks, sin_blocks))
    summed_part = lax.psum_scatter(summed, "img", scatter_dimension=2, tiled=True)
    ref_mass = lax.psum(local_mass, "img")
    new_refs = summed_part / (ref_mass + 1.0)[None, :, None]
    return (new_refs, class_post)


MESH = pl.DeviceIdType.MESH
LANES = 128
CHUNK = 1024
OWNED = 2
PAIRS = SHIFTS // 2
TOGETHER = 4
GROUPS = SHIFTS // TOGETHER
STRIP = 512
CORES = 2
TURN_IN = False
TURN_OUT = True
REF_ROWS = 8


def exchange(src, dst, send_sem, recv_sem, img, ref):
    return pltpu.make_async_remote_copy(
        src_ref=src, dst_ref=dst, send_sem=send_sem, recv_sem=recv_sem, device_id=(img, ref), device_id_type=MESH
    )


def fused_kernel(
    n_img, n_ref,
    images_hbm, references_hbm, precision_hbm, shifts_hbm, labels_hbm, log_prior_hbm,
    new_refs, class_post,
    images, references, precision, shifts, labels, log_prior,
    img_send, img_buf, ref_send, ref_buf, cos_tab, sin_tab, rotated, shifted,
    energy_col, ref_mid, out_mid, part, part_in, own, own_in, post_buf, post_wide, out_send, out_buf, in_sem,
    img_ss, img_rs, ref_ss, ref_rs, part_ss, part_rs, own_ss, own_rs, post_ss, post_rs, out_ss, out_rs,
    ref_mid_ss, ref_mid_rs, out_mid_ss, out_mid_rs,
):
    n_dev = n_img * n_ref
    a = lax.axis_index("img")
    r = lax.axis_index("ref")
    me = a * n_ref + r
    per = n_ref // n_img
    img_dev = images.shape[1]
    n_images = n_img * img_dev
    n_refs = n_ref * REF_ROWS

    loads = [
        pltpu.make_async_copy(src, dst, in_sem.at[i])
        for i, (src, dst) in enumerate(
            (
                (references_hbm, references),
                (images_hbm, images),
                (shifts_hbm, shifts),
                (precision_hbm, precision),
                (labels_hbm, labels),
                (log_prior_hbm, log_prior),
            )
        )
    ]
    for load in loads:
        load.start()

    barrier = pltpu.get_barrier_semaphore()

    def greet(j, carry):
        other = lax.rem(me + j, n_dev)
        pl.semaphore_signal(barrier, inc=1, device_id=(other // n_ref, lax.rem(other, n_ref)), device_id_type=MESH)
        return carry

    lax.fori_loop(1, n_dev, greet, 0)

    loads[0].wait()
    for q in range(n_ref):
        px = pl.ds(q * CHUNK, CHUNK)
        both = jnp.concatenate([references[0, :, px], references[1, :, px]], axis=0)
        ref_send[q] = both.astype(jnp.bfloat16)

    pl.semaphore_wait(barrier, n_dev - 1)

    y, core = a // CORES, lax.rem(a, CORES)
    across = (1 - y) * CORES + core

    def ref_here(q):
        return (lax.rem(q, n_img) == a) & (per * a + q // n_img == r)

    def ref_by_way(q):
        if not TURN_IN:
            return jnp.bool_(False)
        at_mid = (lax.rem(q, n_img) == across) & (per * a + q // n_img == r)
        return (lax.rem(q, n_img) // CORES != y) & jnp.logical_not(at_mid)

    def ref_copy(q):
        return exchange(
            ref_send.at[q], ref_buf.at[r], ref_ss.at[q], ref_rs.at[r], lax.rem(q, n_img), per * a + q // n_img
        )

    def ref_hop(q):
        slot = (q // n_img) * CORES + lax.rem(q, CORES)
        return exchange(ref_send.at[q], ref_mid.at[slot], ref_ss.at[q], ref_mid_rs.at[slot], across, r)

    def ref_start(j, carry):
        q = lax.rem(me + j, n_ref)
        here = ref_here(q)
        by_way = ref_by_way(q)

        @pl.when(here)
        def _():
            ref_buf[r] = ref_send[q]

        @pl.when(by_way)
        def _():
            ref_hop(q).start()

        @pl.when(jnp.logical_not(here | by_way))
        def _():
            ref_copy(q).start()

        return carry

    lax.fori_loop(0, n_ref, ref_start, 0)

    def ref_forward(slot):
        to_img = y * CORES + slot % CORES
        to_ref = per * across + slot // CORES
        return (to_img == a) & (to_ref == r), exchange(
            ref_mid.at[slot], ref_buf.at[r], ref_mid_ss.at[slot], ref_rs.at[r], to_img, to_ref
        )

    loads[1].wait()
    for q in range(n_img):
        img_send[q] = images[:, :, q * CHUNK : (q + 1) * CHUNK].astype(jnp.bfloat16)
    img_buf[a] = img_send[a]
    img_copies = []
    for j in range(1, n_img):
        dest = lax.rem(a + j, n_img)
        copy = exchange(img_send.at[dest], img_buf.at[a], img_ss.at[j], img_rs.at[j], dest, r)
        copy.start()
        img_copies.append(copy)

    if TURN_IN:
        for slot in range(per * CORES):
            stays, copy = ref_forward(slot)

            @pl.when(jnp.logical_not(stays))
            def _():
                exchange(
                    ref_send.at[0], ref_mid.at[slot], ref_ss.at[0], ref_mid_rs.at[slot], across, r
                ).wait_recv()
                copy.start()

    row_first = r * (n_img * CHUNK // COLS) + a * (CHUNK // COLS) - ROWS // 2
    freq_y = lax.broadcasted_iota(jnp.int32, (CHUNK // COLS, COLS), 0) + row_first
    freq_x = lax.broadcasted_iota(jnp.int32, (CHUNK // COLS, COLS), 1)

    for load in loads[2:]:
        load.wait()
    for t in range(SHIFTS):
        turn = freq_x * shifts[0:1, t : t + 1] + freq_y * shifts[1:2, t : t + 1]
        turn = ((turn + ROWS // 2) & (ROWS - 1)) - ROWS // 2
        angle = turn.astype(jnp.float32) * (2.0 * math.pi / ROWS)
        cosine = jnp.cos(angle)
        sine = jnp.sin(angle)
        for n in range(CHUNK // COLS):
            px = slice(n * COLS, (n + 1) * COLS)
            cos_tab[t, :, px] = jnp.broadcast_to(cosine[n : n + 1], (8, COLS))
            sin_tab[t, :, px] = jnp.broadcast_to(sine[n : n + 1], (8, COLS))

    row = lax.broadcasted_iota(jnp.int32, (8, LANES), 0)
    lane = lax.broadcasted_iota(jnp.int32, (8, LANES), 1)
    label_row = jnp.concatenate([labels[...].astype(jnp.float32)] * (LANES // REF_ROWS), axis=1)
    label_row = jnp.where((lane // REF_ROWS) % n_ref == r, jnp.broadcast_to(label_row, (8, LANES)), 0.0)

    for copy in img_copies:
        copy.wait_recv()

    def rotate(t, carry):
        cos_row = cos_tab[t][None]
        sin_row = sin_tab[t][None]
        for b in range(n_img):
            re = img_buf[b, 0].astype(jnp.float32).reshape(img_dev // 8, 8, CHUNK)
            im = img_buf[b, 1].astype(jnp.float32).reshape(img_dev // 8, 8, CHUNK)
            rows = pl.ds(b * img_dev, img_dev)
            turned_re = (re * cos_row - im * sin_row).reshape(img_dev, CHUNK)
            turned_im = (im * cos_row + re * sin_row).reshape(img_dev, CHUNK)
            rotated[t, rows, 0:CHUNK] = turned_re.astype(jnp.bfloat16)
            rotated[t, rows, CHUNK : 2 * CHUNK] = turned_im.astype(jnp.bfloat16)
        return carry

    lax.fori_loop(0, SHIFTS, rotate, 0)

    def arrive(b):
        @pl.when(jnp.logical_not((a == r // per) & (b == r)))
        def _():
            exchange(ref_send.at[0], ref_buf.at[b], ref_ss.at[0], ref_rs.at[b], r // per, b).wait_recv()

    def shift(b, t):
        cos_row = cos_tab[t]
        sin_row = sin_tab[t]
        res = []
        ims = []
        for s in range(2):
            block = ref_buf[b + s].astype(jnp.float32)
            re = block[0:REF_ROWS]
            im = block[REF_ROWS : 2 * REF_ROWS]
            res.append(re * cos_row + im * sin_row)
            ims.append(im * cos_row - re * sin_row)
        rows = pl.ds(pl.multiple_of(b * REF_ROWS, 2 * REF_ROWS), 2 * REF_ROWS)
        shifted[t, rows, 0:CHUNK] = jnp.concatenate(res, axis=0).astype(jnp.bfloat16)
        shifted[t, rows, CHUNK : 2 * CHUNK] = jnp.concatenate(ims, axis=0).astype(jnp.bfloat16)

    def ready(b):
        arrive(b)
        arrive(b + 1)
        for s in range(2):
            block = ref_buf[b + s].astype(jnp.float32)
            square = jnp.sum(block * block, axis=1, keepdims=True)
            square = jnp.broadcast_to(square[0:REF_ROWS] + square[REF_ROWS : 2 * REF_ROWS], (REF_ROWS, LANES))
            energy_col[pl.ds(pl.multiple_of((b + s) * REF_ROWS, REF_ROWS), REF_ROWS)] = square

    layers = n_ref // 2

    def layer_step(i, carry):
        b = 2 * lax.rem(r // 2 + i, layers)
        ready(b)

        def turn_step(t, inner):
            shift(b, t)
            return inner

        return lax.fori_loop(0, SHIFTS, turn_step, carry)

    lax.fori_loop(0, layers - 1, layer_step, 0)
    last = 2 * lax.rem(r // 2 + layers - 1, layers)
    ready(last)
    energy = energy_col[...]
    half_energy = 0.5 * jnp.concatenate([energy, energy], axis=0).T[0:8][None]

    pictures = [img_buf[:, c].reshape(n_images, CHUNK) for c in range(2)]
    pictures = jnp.concatenate(pictures, axis=1)
    part_copies = []
    for g in range(GROUPS):
        for t in range(g * TOGETHER, (g + 1) * TOGETHER):
            shift(last, t)
        group = shifted[g * TOGETHER : (g + 1) * TOGETHER].reshape(TOGETHER * n_refs, 2 * CHUNK)
        cross = inner_rows(pictures, group)
        for h in range(TOGETHER // 2):
            pair = cross[:, h * LANES : (h + 1) * LANES]
            pair = (pair.reshape(n_images // 8, 8, LANES) - half_energy).reshape(n_img, img_dev, LANES)
            part[g, :, :, h * LANES : (h + 1) * LANES] = pair
        for j in range(1, n_img):
            dest = lax.rem(a + j, n_img)
            copy = exchange(
                part.at[g, dest], part_in.at[g, j - 1], part_ss.at[g, j], part_rs.at[g, j], dest, r
            )
            copy.start()
            part_copies.append(copy)

    own[...] = jnp.zeros_like(own)
    own[:, PAIRS, :] = jnp.broadcast_to(label_row[0:1], (img_dev, LANES))
    for copy in part_copies:
        copy.wait_recv()
    for g in range(GROUPS):
        total = part[g, a]
        for j in range(n_img - 1):
            total = total + part_in[g, j]
        for h in range(TOGETHER // 2):
            own[:, g * (TOGETHER // 2) + h, :] = total[:, h * LANES : (h + 1) * LANES]
    own_copies = []
    for j in range(1, n_ref):
        dest = lax.rem(r + j, n_ref)
        copy = exchange(own.at[pl.ds(OWNED * dest, OWNED)], own_in.at[j - 1], own_ss.at[j], own_rs.at[j], a, dest)
        copy.start()
        own_copies.append(copy)
    for copy in own_copies:
        copy.wait_recv()
    mine = own[pl.ds(OWNED * r, OWNED)]
    for j in range(n_ref - 1):
        mine = mine + own_in[j]
    label_lane = jnp.broadcast_to(mine[0, PAIRS : PAIRS + 1], (8, LANES))
    prior = jnp.zeros((8, LANES), jnp.float32)
    for c in range(CLASSES):
        prior = prior + jnp.where(label_lane == c, log_prior[:, c : c + 1], 0.0)
    image_lane = lax.broadcasted_iota(jnp.int32, (1, img_dev), 1)

    blocks = []
    for il in range(OWNED):
        noise = jnp.sum(jnp.where(image_lane == OWNED * r + il, precision[...], 0.0), axis=1, keepdims=True)
        scores = noise * mine[il] + prior
        scores = jnp.where(row < PAIRS, scores, -jnp.inf)
        top = jnp.max(jnp.max(scores, axis=1, keepdims=True), axis=0, keepdims=True)
        exponent = jnp.exp(scores - top)
        row_total = jnp.sum(jnp.sum(exponent, axis=1, keepdims=True), axis=0, keepdims=True)
        posterior = exponent / row_total
        lane_sum = jnp.broadcast_to(jnp.sum(posterior, axis=0, keepdims=True), (8, LANES))
        totals = lane_sum + pltpu.roll(lane_sum, n_refs, 1)
        for c in range(CLASSES):
            in_class = jnp.sum(jnp.where(label_lane == c, lane_sum, 0.0), axis=1, keepdims=True)
            totals = jnp.where(lane == n_refs + c, in_class, totals)
        high = totals.astype(jnp.bfloat16).astype(jnp.float32)
        block = jnp.where(row == PAIRS, high, posterior)
        blocks.append(jnp.where(row == PAIRS + 1, totals - high, block))
    post_buf[me] = jnp.concatenate(blocks, axis=0).astype(jnp.bfloat16)

    def post_copy(j):
        other = lax.rem(me + j, n_dev)
        return exchange(
            post_buf.at[me], post_buf.at[me], post_ss.at[j], post_rs.at[j], other // n_ref, lax.rem(other, n_ref)
        )

    def post_start(j, carry):
        post_copy(j).start()
        return carry

    lax.fori_loop(1, n_dev, post_start, 0)

    def post_arrive(j, carry):
        source = lax.rem(me + n_dev - j, n_dev)
        exchange(
            post_buf.at[me], post_buf.at[source], post_ss.at[j], post_rs.at[j], source // n_ref, lax.rem(source, n_ref)
        ).wait_recv()
        return carry

    lax.fori_loop(1, n_dev, post_arrive, 0)

    post_wide[...] = post_buf[...].astype(jnp.float32).reshape(n_images, 8, LANES)
    totals = post_wide[:, PAIRS, :] + post_wide[:, PAIRS + 1, :]
    mass = jnp.broadcast_to(jnp.sum(totals, axis=0, keepdims=True), (LANES, LANES)).T[0:n_refs]
    scale = 1.0 / (mass[:, 0:1] + 1.0)
    first = pl.ds(a * img_dev, img_dev)
    mine = post_wide[first, PAIRS, :] + post_wide[first, PAIRS + 1, :]
    class_post[...] = jnp.concatenate([mine] * (LANES // img_dev), axis=0).T[n_refs : n_refs + CLASSES, 0:img_dev]
    weights = []
    for tp in range(PAIRS):
        both = post_wide[:, tp, :].T
        weights.append(jnp.concatenate([both[0:n_refs], both[n_refs : 2 * n_refs]], axis=1).astype(jnp.bfloat16))
    weights = jnp.concatenate(weights, axis=1)
    turned = rotated[...].reshape(SHIFTS * n_images, 2 * CHUNK)
    piece = lax.rem(r, per) * n_img + a

    target = r // per
    turned_y = target // CORES != y
    middle = y * CORES + lax.rem(target, CORES)

    def out_by_way(j):
        if not TURN_OUT:
            return jnp.bool_(False)
        return turned_y & jnp.logical_not((middle == a) & (j == r))

    def out_copy(h, j):
        return exchange(
            out_send.at[h, j], out_buf.at[h, piece], out_ss.at[h, j], out_rs.at[h, piece], target, j
        )

    def out_hop(h, j):
        slot = core * per + lax.rem(r, per)
        return exchange(
            out_send.at[h, j], out_mid.at[h, slot], out_ss.at[h, j], out_mid_rs.at[h, slot], middle, j
        )

    def out_forward(h, slot):
        from_img = y * CORES + slot // per
        from_ref = per * across + slot % per
        arrived = (slot % per) * n_img + from_img
        return (from_img == a) & (from_ref == r), exchange(
            out_mid.at[h, slot], out_buf.at[h, arrived], out_mid_ss.at[h, slot], out_rs.at[h, arrived], across, r
        )

    for h in range(CHUNK // STRIP):
        real = jnp.dot(weights, turned[:, h * STRIP : (h + 1) * STRIP], preferred_element_type=jnp.float32)
        imag = jnp.dot(
            weights, turned[:, CHUNK + h * STRIP : CHUNK + (h + 1) * STRIP], preferred_element_type=jnp.float32
        )
        real = (real * scale).reshape(n_ref, REF_ROWS, STRIP)
        imag = (imag * scale).reshape(n_ref, REF_ROWS, STRIP)
        out_send[h] = jnp.concatenate([real, imag], axis=1).astype(jnp.bfloat16)

        def out_start(i, carry):
            j = lax.rem(r + i, n_ref)
            here = (a == target) & (j == r)
            by_way = out_by_way(j)

            @pl.when(here)
            def _():
                out_buf[h, piece] = out_send[h, j]

            @pl.when(by_way)
            def _():
                out_hop(h, j).start()

            @pl.when(jnp.logical_not(here | by_way))
            def _():
                out_copy(h, j).start()

            return carry

        lax.fori_loop(0, n_ref, out_start, 0)

    if TURN_OUT:
        for h in range(CHUNK // STRIP):
            for slot in range(per * CORES):
                stays, copy = out_forward(h, slot)

                @pl.when(jnp.logical_not(stays))
                def _():
                    exchange(
                        out_send.at[h, 0], out_mid.at[h, slot], out_ss.at[h, 0], out_mid_rs.at[h, slot], a, 0
                    ).wait_recv()
                    copy.start()

    for h in range(CHUNK // STRIP):
        for q in range(n_ref):
            @pl.when(jnp.logical_not(ref_here(q)))
            def _():
                exchange(
                    out_send.at[h, 0], out_buf.at[h, q], out_ss.at[h, 0], out_rs.at[h, q],
                    q % n_img, per * a + q // n_img,
                ).wait_recv()

            new_refs[:, q * CHUNK + h * STRIP : q * CHUNK + (h + 1) * STRIP] = out_buf[h, q]

    for copy in img_copies + part_copies + own_copies:
        copy.wait_send()

    def post_sent(j, carry):
        post_copy(j).wait_send()
        return carry

    lax.fori_loop(1, n_dev, post_sent, 0)

    def edge_sent(j, carry):
        @pl.when(jnp.logical_not(ref_here(j)))
        def _():
            ref_copy(j).wait_send()

        @pl.when(jnp.logical_not((a == r // per) & (j == r)))
        def _():
            for h in range(CHUNK // STRIP):
                out_copy(h, j).wait_send()

        return carry

    lax.fori_loop(0, n_ref, edge_sent, 0)
    for slot in range(per * CORES):
        if TURN_IN:
            stays, copy = ref_forward(slot)

            @pl.when(jnp.logical_not(stays))
            def _():
                copy.wait_send()

        if TURN_OUT:
            for h in range(CHUNK // STRIP):
                stays, copy = out_forward(h, slot)

                @pl.when(jnp.logical_not(stays))
                def _():
                    copy.wait_send()


def fused(n_img, n_ref, images, references, precision, shifts, labels, log_prior):
    img_dev = images.shape[1]
    n_images = n_img * img_dev
    n_refs = n_ref * REF_ROWS
    n_dev = n_img * n_ref
    vmem = pl.BlockSpec(memory_space=pltpu.VMEM)
    far = pl.BlockSpec(memory_space=pl.ANY)
    low = jnp.bfloat16
    wide = jnp.float32
    strips = CHUNK // STRIP
    per = n_ref // n_img
    parts = (GROUPS, n_img)
    outs = (strips, n_ref)
    counts = ((6,), (n_img,), (n_img,), (n_ref,), (n_ref,), parts, parts)
    counts = counts + ((n_ref,), (n_ref,), (n_dev,), (n_dev,), outs, outs)
    mids = (strips, CORES * per)
    counts = counts + ((CORES * per,), (CORES * per,), mids, mids)
    new_refs, class_rows = pl.pallas_call(
        functools.partial(fused_kernel, n_img, n_ref),
        out_shape=(
            jax.ShapeDtypeStruct((2 * REF_ROWS, references.shape[2]), low),
            jax.ShapeDtypeStruct((CLASSES, img_dev), wide),
        ),
        in_specs=[far] * 6,
        out_specs=(vmem, vmem),
        scratch_shapes=[
            pltpu.VMEM(images.shape, wide),
            pltpu.VMEM(references.shape, wide),
            pltpu.VMEM((1, img_dev), wide),
            pltpu.VMEM((2, SHIFTS), jnp.int32),
            pltpu.VMEM((1, REF_ROWS), jnp.int32),
            pltpu.VMEM((1, CLASSES), wide),
            pltpu.VMEM((n_img, 2, img_dev, CHUNK), low),
            pltpu.VMEM((n_img, 2, img_dev, CHUNK), low),
            pltpu.VMEM((n_ref, 2 * REF_ROWS, CHUNK), low),
            pltpu.VMEM((n_ref, 2 * REF_ROWS, CHUNK), low),
            pltpu.VMEM((SHIFTS, 8, CHUNK), wide),
            pltpu.VMEM((SHIFTS, 8, CHUNK), wide),
            pltpu.VMEM((SHIFTS, n_images, 2 * CHUNK), low),
            pltpu.VMEM((SHIFTS, n_refs, 2 * CHUNK), low),
            pltpu.VMEM((n_refs, LANES), wide),
            pltpu.VMEM((CORES * per, 2 * REF_ROWS, CHUNK), low),
            pltpu.VMEM((strips, CORES * per, 2 * REF_ROWS, STRIP), low),
            pltpu.VMEM((GROUPS, n_img, img_dev, TOGETHER * n_refs), wide),
            pltpu.VMEM((GROUPS, n_img - 1, img_dev, TOGETHER * n_refs), wide),
            pltpu.VMEM((img_dev, 8, LANES), wide),
            pltpu.VMEM((n_ref - 1, OWNED, 8, LANES), wide),
            pltpu.VMEM((n_dev, 16, LANES), low),
            pltpu.VMEM((n_images, 8, LANES), wide),
            pltpu.VMEM((strips, n_ref, 2 * REF_ROWS, STRIP), low),
            pltpu.VMEM((strips, n_ref, 2 * REF_ROWS, STRIP), low),
        ]
        + [pltpu.SemaphoreType.DMA(count) for count in counts],
        compiler_params=pltpu.CompilerParams(
            collective_id=0, has_side_effects=True, vmem_limit_bytes=56 * 1024 * 1024
        ),
        cost_estimate=pl.CostEstimate(flops=800_000_000, bytes_accessed=2_000_000, transcendentals=25_000),
    )(
        images,
        references,
        precision.reshape(1, img_dev),
        shifts.T,
        labels.reshape(1, REF_ROWS),
        log_prior.reshape(1, CLASSES),
    )
    return new_refs.reshape(references.shape).astype(wide), class_rows.T


def local(n_img, n_ref, images, references, precision, shifts, labels, log_prior):
    fits = (
        images.shape[1] == OWNED * n_ref
        and images.shape[1] % 16 == 0
        and references.shape[1] == REF_ROWS
        and 2 * n_ref * REF_ROWS == LANES
        and images.shape[2] == n_img * CHUNK
        and references.shape[2] == n_ref * CHUNK
        and n_ref % n_img == 0
        and n_img == 2 * CORES
    )
    if fits:
        return fused(n_img, n_ref, images, references, precision, shifts, labels, log_prior)
    return gathered(images, references, precision, shifts, labels, log_prior)


def solution(mesh):
    return jax.shard_map(
        functools.partial(local, mesh.shape["img"], mesh.shape["ref"]),
        mesh=mesh,
        in_specs=(P(None, "img", "ref"), P(None, "ref", "img"), P("img"), P(), P("ref"), P()),
        out_specs=(P(None, "ref", "img"), P("img", None)),
        check_vma=False,
    )
```

```python
import functools
import math

import jax
import jax.numpy as jnp
from jax import lax
from jax.experimental import pallas as pl
from jax.experimental.pallas import tpu as pltpu
from jax.sharding import PartitionSpec as P

ROWS = 256
COLS = 128
SHIFTS = 12
CLASSES = 4


def phases(shifts):
    index = jnp.arange(ROWS * COLS, dtype=jnp.int32)
    freq_y = (index // COLS - ROWS // 2).astype(jnp.float32)
    freq_x = (index % COLS).astype(jnp.float32)
    shift_x = shifts[:, 0].astype(jnp.float32)[:, None]
    shift_y = shifts[:, 1].astype(jnp.float32)[:, None]
    angles = 2.0 * math.pi / ROWS * (freq_x[None, :] * shift_x + freq_y[None, :] * shift_y)
    return (jnp.cos(angles), jnp.sin(angles))


def inner_rows(left, right):
    return lax.dot_general(
        left, right, (((1,), (1,)), ((), ())), preferred_element_type=jnp.float32
    )


def inner_cols(left, right):
    return lax.dot_general(
        left, right, (((0,), (0,)), ((), ())), preferred_element_type=jnp.float32
    )


def gathered(images, references, precision, shifts, labels, log_prior):
    img_low = lax.all_gather(images.astype(jnp.bfloat16), "ref", axis=2, tiled=True)
    ref_low = lax.all_gather(references.astype(jnp.bfloat16), "img", axis=2, tiled=True)
    pixels = img_low.shape[2]
    img_dev = img_low.shape[1]
    ref_dev = ref_low.shape[1]
    blocks = SHIFTS // 4
    cosine, sine_part = phases(shifts)
    cos_blocks = cosine.reshape(blocks, 4, pixels)
    sin_blocks = sine_part.reshape(blocks, 4, pixels)
    ref_wide = ref_low.astype(jnp.float32)
    energy = jnp.sum(ref_wide * ref_wide, axis=(0, 2))
    onehot = (labels[:, None] == jnp.arange(CLASSES, dtype=jnp.int32)[None, :]).astype(jnp.float32)
    prior_term = jnp.sum(onehot * log_prior[None, :], axis=1)

    def cross_block(operands):
        cos_rows, sin_rows = operands
        shifted_re = (
            ref_wide[0][None] * cos_rows[:, None, :] + ref_wide[1][None] * sin_rows[:, None, :]
        ).astype(jnp.bfloat16)
        shifted_im = (
            ref_wide[1][None] * cos_rows[:, None, :] - ref_wide[0][None] * sin_rows[:, None, :]
        ).astype(jnp.bfloat16)
        return inner_rows(img_low[0], shifted_re.reshape(4 * ref_dev, pixels)) + inner_rows(
            img_low[1], shifted_im.reshape(4 * ref_dev, pixels)
        )

    cross_terms = lax.map(cross_block, (cos_blocks, sin_blocks))
    cross_terms = jnp.transpose(cross_terms, (1, 0, 2)).reshape(img_dev, SHIFTS, ref_dev)
    scores = (
        precision[:, None, None] * (cross_terms - 0.5 * energy[None, None, :])
        + prior_term[None, None, :]
    )
    local_top = jnp.max(scores, axis=(1, 2))
    top_score = lax.pmax(local_top, "ref")
    exponent = jnp.exp(scores - top_score[:, None, None])
    local_class = jnp.einsum(
        "ik,kc->ic", jnp.sum(exponent, axis=1), onehot, precision=lax.Precision.HIGHEST
    )
    row_total, class_sum = lax.psum((jnp.sum(exponent, axis=(1, 2)), local_class), "ref")
    posterior = exponent / row_total[:, None, None]
    class_post = class_sum / row_total[:, None]
    local_mass = jnp.sum(posterior, axis=(0, 1))
    post_low = posterior.astype(jnp.bfloat16).reshape(img_dev, blocks, 4 * ref_dev)
    post_low = jnp.transpose(post_low, (1, 0, 2))

    def back_block(running, operands):
        weights_blk, cos_rows, sin_rows = operands
        back_re = inner_cols(weights_blk, img_low[0]).reshape(4, ref_dev, pixels)
        back_im = inner_cols(weights_blk, img_low[1]).reshape(4, ref_dev, pixels)
        part_re = jnp.sum(back_re * cos_rows[:, None, :] - back_im * sin_rows[:, None, :], axis=0)
        part_im = jnp.sum(back_im * cos_rows[:, None, :] + back_re * sin_rows[:, None, :], axis=0)
        return (running + jnp.stack([part_re, part_im]), None)

    start_sum = jnp.zeros((2, ref_dev, pixels), jnp.float32)
    summed, unused = lax.scan(back_block, start_sum, (post_low, cos_blocks, sin_blocks))
    summed_part = lax.psum_scatter(summed, "img", scatter_dimension=2, tiled=True)
    ref_mass = lax.psum(local_mass, "img")
    new_refs = summed_part / (ref_mass + 1.0)[None, :, None]
    return (new_refs, class_post)


MESH = pl.DeviceIdType.MESH
LANES = 128
CHUNK = 1024
OWNED = 2
PAIRS = SHIFTS // 2
TOGETHER = 4
GROUPS = SHIFTS // TOGETHER
STRIP = 512
CORES = 2
TURN_IN = True
TURN_OUT = False
REF_ROWS = 8


def exchange(src, dst, send_sem, recv_sem, img, ref):
    return pltpu.make_async_remote_copy(
        src_ref=src, dst_ref=dst, send_sem=send_sem, recv_sem=recv_sem, device_id=(img, ref), device_id_type=MESH
    )


def fused_kernel(
    n_img, n_ref,
    images_hbm, references_hbm, precision_hbm, shifts_hbm, labels_hbm, log_prior_hbm,
    new_refs, class_post,
    images, references, precision, shifts, labels, log_prior,
    img_send, img_buf, ref_send, ref_buf, cos_tab, sin_tab, rotated, shifted,
    energy_col, ref_mid, out_mid, part, part_in, own, own_in, post_buf, post_wide, out_send, out_buf, in_sem,
    img_ss, img_rs, ref_ss, ref_rs, part_ss, part_rs, own_ss, own_rs, post_ss, post_rs, out_ss, out_rs,
    ref_mid_ss, ref_mid_rs, out_mid_ss, out_mid_rs,
):
    n_dev = n_img * n_ref
    a = lax.axis_index("img")
    r = lax.axis_index("ref")
    me = a * n_ref + r
    per = n_ref // n_img
    img_dev = images.shape[1]
    n_images = n_img * img_dev
    n_refs = n_ref * REF_ROWS

    loads = [
        pltpu.make_async_copy(src, dst, in_sem.at[i])
        for i, (src, dst) in enumerate(
            (
                (references_hbm, references),
                (images_hbm, images),
                (shifts_hbm, shifts),
                (precision_hbm, precision),
                (labels_hbm, labels),
                (log_prior_hbm, log_prior),
            )
        )
    ]
    for load in loads:
        load.start()

    barrier = pltpu.get_barrier_semaphore()

    def greet(j, carry):
        other = lax.rem(me + j, n_dev)
        pl.semaphore_signal(barrier, inc=1, device_id=(other // n_ref, lax.rem(other, n_ref)), device_id_type=MESH)
        return carry

    lax.fori_loop(1, n_dev, greet, 0)

    loads[0].wait()
    for q in range(n_ref):
        px = pl.ds(q * CHUNK, CHUNK)
        both = jnp.concatenate([references[0, :, px], references[1, :, px]], axis=0)
        ref_send[q] = both.astype(jnp.bfloat16)

    pl.semaphore_wait(barrier, n_dev - 1)

    y, core = a // CORES, lax.rem(a, CORES)
    across = (1 - y) * CORES + core

    def ref_here(q):
        return (lax.rem(q, n_img) == a) & (per * a + q // n_img == r)

    def ref_by_way(q):
        if not TURN_IN:
            return jnp.bool_(False)
        at_mid = (lax.rem(q, n_img) == across) & (per * a + q // n_img == r)
        return (lax.rem(q, n_img) // CORES != y) & jnp.logical_not(at_mid)

    def ref_copy(q):
        return exchange(
            ref_send.at[q], ref_buf.at[r], ref_ss.at[q], ref_rs.at[r], lax.rem(q, n_img), per * a + q // n_img
        )

    def ref_hop(q):
        slot = (q // n_img) * CORES + lax.rem(q, CORES)
        return exchange(ref_send.at[q], ref_mid.at[slot], ref_ss.at[q], ref_mid_rs.at[slot], across, r)

    def ref_start(j, carry):
        q = lax.rem(me + j, n_ref)
        here = ref_here(q)
        by_way = ref_by_way(q)

        @pl.when(here)
        def _():
            ref_buf[r] = ref_send[q]

        @pl.when(by_way)
        def _():
            ref_hop(q).start()

        @pl.when(jnp.logical_not(here | by_way))
        def _():
            ref_copy(q).start()

        return carry

    lax.fori_loop(0, n_ref, ref_start, 0)

    def ref_forward(slot):
        to_img = y * CORES + slot % CORES
        to_ref = per * across + slot // CORES
        return (to_img == a) & (to_ref == r), exchange(
            ref_mid.at[slot], ref_buf.at[r], ref_mid_ss.at[slot], ref_rs.at[r], to_img, to_ref
        )

    loads[1].wait()
    for q in range(n_img):
        img_send[q] = images[:, :, q * CHUNK : (q + 1) * CHUNK].astype(jnp.bfloat16)
    img_buf[a] = img_send[a]
    img_copies = []
    for j in range(1, n_img):
        dest = lax.rem(a + j, n_img)
        copy = exchange(img_send.at[dest], img_buf.at[a], img_ss.at[j], img_rs.at[j], dest, r)
        copy.start()
        img_copies.append(copy)

    if TURN_IN:
        for slot in range(per * CORES):
            stays, copy = ref_forward(slot)

            @pl.when(jnp.logical_not(stays))
            def _():
                exchange(
                    ref_send.at[0], ref_mid.at[slot], ref_ss.at[0], ref_mid_rs.at[slot], across, r
                ).wait_recv()
                copy.start()

    row_first = r * (n_img * CHUNK // COLS) + a * (CHUNK // COLS) - ROWS // 2
    freq_y = lax.broadcasted_iota(jnp.int32, (CHUNK // COLS, COLS), 0) + row_first
    freq_x = lax.broadcasted_iota(jnp.int32, (CHUNK // COLS, COLS), 1)

    for load in loads[2:]:
        load.wait()
    for t in range(SHIFTS):
        turn = freq_x * shifts[0:1, t : t + 1] + freq_y * shifts[1:2, t : t + 1]
        turn = ((turn + ROWS // 2) & (ROWS - 1)) - ROWS // 2
        angle = turn.astype(jnp.float32) * (2.0 * math.pi / ROWS)
        cosine = jnp.cos(angle)
        sine = jnp.sin(angle)
        for n in range(CHUNK // COLS):
            px = slice(n * COLS, (n + 1) * COLS)
            cos_tab[t, :, px] = jnp.broadcast_to(cosine[n : n + 1], (8, COLS))
            sin_tab[t, :, px] = jnp.broadcast_to(sine[n : n + 1], (8, COLS))

    row = lax.broadcasted_iota(jnp.int32, (8, LANES), 0)
    lane = lax.broadcasted_iota(jnp.int32, (8, LANES), 1)
    label_row = jnp.concatenate([labels[...].astype(jnp.float32)] * (LANES // REF_ROWS), axis=1)
    label_row = jnp.where((lane // REF_ROWS) % n_ref == r, jnp.broadcast_to(label_row, (8, LANES)), 0.0)

    for copy in img_copies:
        copy.wait_recv()

    def rotate(t, carry):
        cos_row = cos_tab[t][None]
        sin_row = sin_tab[t][None]
        for b in range(n_img):
            re = img_buf[b, 0].astype(jnp.float32).reshape(img_dev // 8, 8, CHUNK)
            im = img_buf[b, 1].astype(jnp.float32).reshape(img_dev // 8, 8, CHUNK)
            rows = pl.ds(b * img_dev, img_dev)
            turned_re = (re * cos_row - im * sin_row).reshape(img_dev, CHUNK)
            turned_im = (im * cos_row + re * sin_row).reshape(img_dev, CHUNK)
            rotated[t, rows, 0:CHUNK] = turned_re.astype(jnp.bfloat16)
            rotated[t, rows, CHUNK : 2 * CHUNK] = turned_im.astype(jnp.bfloat16)
        return carry

    lax.fori_loop(0, SHIFTS, rotate, 0)

    def arrive(b):
        @pl.when(jnp.logical_not((a == r // per) & (b == r)))
        def _():
            exchange(ref_send.at[0], ref_buf.at[b], ref_ss.at[0], ref_rs.at[b], r // per, b).wait_recv()

    def shift(b, t):
        cos_row = cos_tab[t]
        sin_row = sin_tab[t]
        res = []
        ims = []
        for s in range(2):
            block = ref_buf[b + s].astype(jnp.float32)
            re = block[0:REF_ROWS]
            im = block[REF_ROWS : 2 * REF_ROWS]
            res.append(re * cos_row + im * sin_row)
            ims.append(im * cos_row - re * sin_row)
        rows = pl.ds(pl.multiple_of(b * REF_ROWS, 2 * REF_ROWS), 2 * REF_ROWS)
        shifted[t, rows, 0:CHUNK] = jnp.concatenate(res, axis=0).astype(jnp.bfloat16)
        shifted[t, rows, CHUNK : 2 * CHUNK] = jnp.concatenate(ims, axis=0).astype(jnp.bfloat16)

    def ready(b):
        arrive(b)
        arrive(b + 1)
        for s in range(2):
            block = ref_buf[b + s].astype(jnp.float32)
            square = jnp.sum(block * block, axis=1, keepdims=True)
            square = jnp.broadcast_to(square[0:REF_ROWS] + square[REF_ROWS : 2 * REF_ROWS], (REF_ROWS, LANES))
            energy_col[pl.ds(pl.multiple_of((b + s) * REF_ROWS, REF_ROWS), REF_ROWS)] = square

    layers = n_ref // 2

    def layer_step(i, carry):
        b = 2 * lax.rem(r // 2 + i, layers)
        ready(b)

        def turn_step(t, inner):
            shift(b, t)
            return inner

        return lax.fori_loop(0, SHIFTS, turn_step, carry)

    lax.fori_loop(0, layers - 1, layer_step, 0)
    last = 2 * lax.rem(r // 2 + layers - 1, layers)
    ready(last)
    energy = energy_col[...]
    half_energy = 0.5 * jnp.concatenate([energy, energy], axis=0).T[0:8][None]

    pictures = [img_buf[:, c].reshape(n_images, CHUNK) for c in range(2)]
    pictures = jnp.concatenate(pictures, axis=1)
    part_copies = []
    for g in range(GROUPS):
        for t in range(g * TOGETHER, (g + 1) * TOGETHER):
            shift(last, t)
        group = shifted[g * TOGETHER : (g + 1) * TOGETHER].reshape(TOGETHER * n_refs, 2 * CHUNK)
        cross = inner_rows(pictures, group)
        for h in range(TOGETHER // 2):
            pair = cross[:, h * LANES : (h + 1) * LANES]
            pair = (pair.reshape(n_images // 8, 8, LANES) - half_energy).reshape(n_img, img_dev, LANES)
            part[g, :, :, h * LANES : (h + 1) * LANES] = pair
        for j in range(1, n_img):
            dest = lax.rem(a + j, n_img)
            copy = exchange(
                part.at[g, dest], part_in.at[g, j - 1], part_ss.at[g, j], part_rs.at[g, j], dest, r
            )
            copy.start()
            part_copies.append(copy)

    own[...] = jnp.zeros_like(own)
    own[:, PAIRS, :] = jnp.broadcast_to(label_row[0:1], (img_dev, LANES))
    for copy in part_copies:
        copy.wait_recv()
    for g in range(GROUPS):
        total = part[g, a]
        for j in range(n_img - 1):
            total = total + part_in[g, j]
        for h in range(TOGETHER // 2):
            own[:, g * (TOGETHER // 2) + h, :] = total[:, h * LANES : (h + 1) * LANES]
    own_copies = []
    for j in range(1, n_ref):
        dest = lax.rem(r + j, n_ref)
        copy = exchange(own.at[pl.ds(OWNED * dest, OWNED)], own_in.at[j - 1], own_ss.at[j], own_rs.at[j], a, dest)
        copy.start()
        own_copies.append(copy)
    for copy in own_copies:
        copy.wait_recv()
    mine = own[pl.ds(OWNED * r, OWNED)]
    for j in range(n_ref - 1):
        mine = mine + own_in[j]
    label_lane = jnp.broadcast_to(mine[0, PAIRS : PAIRS + 1], (8, LANES))
    prior = jnp.zeros((8, LANES), jnp.float32)
    for c in range(CLASSES):
        prior = prior + jnp.where(label_lane == c, log_prior[:, c : c + 1], 0.0)
    image_lane = lax.broadcasted_iota(jnp.int32, (1, img_dev), 1)

    blocks = []
    for il in range(OWNED):
        noise = jnp.sum(jnp.where(image_lane == OWNED * r + il, precision[...], 0.0), axis=1, keepdims=True)
        scores = noise * mine[il] + prior
        scores = jnp.where(row < PAIRS, scores, -jnp.inf)
        top = jnp.max(jnp.max(scores, axis=1, keepdims=True), axis=0, keepdims=True)
        exponent = jnp.exp(scores - top)
        row_total = jnp.sum(jnp.sum(exponent, axis=1, keepdims=True), axis=0, keepdims=True)
        posterior = exponent / row_total
        lane_sum = jnp.broadcast_to(jnp.sum(posterior, axis=0, keepdims=True), (8, LANES))
        totals = lane_sum + pltpu.roll(lane_sum, n_refs, 1)
        for c in range(CLASSES):
            in_class = jnp.sum(jnp.where(label_lane == c, lane_sum, 0.0), axis=1, keepdims=True)
            totals = jnp.where(lane == n_refs + c, in_class, totals)
        high = totals.astype(jnp.bfloat16).astype(jnp.float32)
        block = jnp.where(row == PAIRS, high, posterior)
        blocks.append(jnp.where(row == PAIRS + 1, totals - high, block))
    post_buf[me] = jnp.concatenate(blocks, axis=0).astype(jnp.bfloat16)

    def post_copy(j):
        other = lax.rem(me + j, n_dev)
        return exchange(
            post_buf.at[me], post_buf.at[me], post_ss.at[j], post_rs.at[j], other // n_ref, lax.rem(other, n_ref)
        )

    def post_start(j, carry):
        post_copy(j).start()
        return carry

    lax.fori_loop(1, n_dev, post_start, 0)

    def post_arrive(j, carry):
        source = lax.rem(me + n_dev - j, n_dev)
        exchange(
            post_buf.at[me], post_buf.at[source], post_ss.at[j], post_rs.at[j], source // n_ref, lax.rem(source, n_ref)
        ).wait_recv()
        return carry

    lax.fori_loop(1, n_dev, post_arrive, 0)

    post_wide[...] = post_buf[...].astype(jnp.float32).reshape(n_images, 8, LANES)
    totals = post_wide[:, PAIRS, :] + post_wide[:, PAIRS + 1, :]
    mass = jnp.broadcast_to(jnp.sum(totals, axis=0, keepdims=True), (LANES, LANES)).T[0:n_refs]
    scale = 1.0 / (mass[:, 0:1] + 1.0)
    first = pl.ds(a * img_dev, img_dev)
    mine = post_wide[first, PAIRS, :] + post_wide[first, PAIRS + 1, :]
    class_post[...] = jnp.concatenate([mine] * (LANES // img_dev), axis=0).T[n_refs : n_refs + CLASSES, 0:img_dev]
    weights = []
    for tp in range(PAIRS):
        both = post_wide[:, tp, :].T
        weights.append(jnp.concatenate([both[0:n_refs], both[n_refs : 2 * n_refs]], axis=1).astype(jnp.bfloat16))
    weights = jnp.concatenate(weights, axis=1)
    turned = rotated[...].reshape(SHIFTS * n_images, 2 * CHUNK)
    piece = lax.rem(r, per) * n_img + a

    target = r // per
    turned_y = target // CORES != y
    middle = y * CORES + lax.rem(target, CORES)

    def out_by_way(j):
        if not TURN_OUT:
            return jnp.bool_(False)
        return turned_y & jnp.logical_not((middle == a) & (j == r))

    def out_copy(h, j):
        return exchange(
            out_send.at[h, j], out_buf.at[h, piece], out_ss.at[h, j], out_rs.at[h, piece], target, j
        )

    def out_hop(h, j):
        slot = core * per + lax.rem(r, per)
        return exchange(
            out_send.at[h, j], out_mid.at[h, slot], out_ss.at[h, j], out_mid_rs.at[h, slot], middle, j
        )

    def out_forward(h, slot):
        from_img = y * CORES + slot // per
        from_ref = per * across + slot % per
        arrived = (slot % per) * n_img + from_img
        return (from_img == a) & (from_ref == r), exchange(
            out_mid.at[h, slot], out_buf.at[h, arrived], out_mid_ss.at[h, slot], out_rs.at[h, arrived], across, r
        )

    for h in range(CHUNK // STRIP):
        real = jnp.dot(weights, turned[:, h * STRIP : (h + 1) * STRIP], preferred_element_type=jnp.float32)
        imag = jnp.dot(
            weights, turned[:, CHUNK + h * STRIP : CHUNK + (h + 1) * STRIP], preferred_element_type=jnp.float32
        )
        real = (real * scale).reshape(n_ref, REF_ROWS, STRIP)
        imag = (imag * scale).reshape(n_ref, REF_ROWS, STRIP)
        out_send[h] = jnp.concatenate([real, imag], axis=1).astype(jnp.bfloat16)

        def out_start(i, carry):
            j = lax.rem(r + i, n_ref)
            here = (a == target) & (j == r)
            by_way = out_by_way(j)

            @pl.when(here)
            def _():
                out_buf[h, piece] = out_send[h, j]

            @pl.when(by_way)
            def _():
                out_hop(h, j).start()

            @pl.when(jnp.logical_not(here | by_way))
            def _():
                out_copy(h, j).start()

            return carry

        lax.fori_loop(0, n_ref, out_start, 0)

    if TURN_OUT:
        for h in range(CHUNK // STRIP):
            for slot in range(per * CORES):
                stays, copy = out_forward(h, slot)

                @pl.when(jnp.logical_not(stays))
                def _():
                    exchange(
                        out_send.at[h, 0], out_mid.at[h, slot], out_ss.at[h, 0], out_mid_rs.at[h, slot], a, 0
                    ).wait_recv()
                    copy.start()

    for h in range(CHUNK // STRIP):
        for q in range(n_ref):
            @pl.when(jnp.logical_not(ref_here(q)))
            def _():
                exchange(
                    out_send.at[h, 0], out_buf.at[h, q], out_ss.at[h, 0], out_rs.at[h, q],
                    q % n_img, per * a + q // n_img,
                ).wait_recv()

            new_refs[:, q * CHUNK + h * STRIP : q * CHUNK + (h + 1) * STRIP] = out_buf[h, q]

    for copy in img_copies + part_copies + own_copies:
        copy.wait_send()

    def post_sent(j, carry):
        post_copy(j).wait_send()
        return carry

    lax.fori_loop(1, n_dev, post_sent, 0)

    def edge_sent(j, carry):
        @pl.when(jnp.logical_not(ref_here(j)))
        def _():
            ref_copy(j).wait_send()

        @pl.when(jnp.logical_not((a == r // per) & (j == r)))
        def _():
            for h in range(CHUNK // STRIP):
                out_copy(h, j).wait_send()

        return carry

    lax.fori_loop(0, n_ref, edge_sent, 0)
    for slot in range(per * CORES):
        if TURN_IN:
            stays, copy = ref_forward(slot)

            @pl.when(jnp.logical_not(stays))
            def _():
                copy.wait_send()

        if TURN_OUT:
            for h in range(CHUNK // STRIP):
                stays, copy = out_forward(h, slot)

                @pl.when(jnp.logical_not(stays))
                def _():
                    copy.wait_send()


def widen_kernel(low, class_rows, new_refs, class_post):
    for q in range(low.shape[1] // CHUNK):
        px = slice(q * CHUNK, (q + 1) * CHUNK)
        block = low[:, px].astype(jnp.float32)
        new_refs[0, :, px] = block[0:REF_ROWS]
        new_refs[1, :, px] = block[REF_ROWS : 2 * REF_ROWS]
    class_post[...] = class_rows[...]


def fused(n_img, n_ref, images, references, precision, shifts, labels, log_prior):
    img_dev = images.shape[1]
    n_images = n_img * img_dev
    n_refs = n_ref * REF_ROWS
    n_dev = n_img * n_ref
    vmem = pl.BlockSpec(memory_space=pltpu.VMEM)
    far = pl.BlockSpec(memory_space=pl.ANY)
    low = jnp.bfloat16
    wide = jnp.float32
    strips = CHUNK // STRIP
    per = n_ref // n_img
    parts = (GROUPS, n_img)
    outs = (strips, n_ref)
    counts = ((6,), (n_img,), (n_img,), (n_ref,), (n_ref,), parts, parts)
    counts = counts + ((n_ref,), (n_ref,), (n_dev,), (n_dev,), outs, outs)
    mids = (strips, CORES * per)
    counts = counts + ((CORES * per,), (CORES * per,), mids, mids)
    new_refs, class_rows = pl.pallas_call(
        functools.partial(fused_kernel, n_img, n_ref),
        out_shape=(
            jax.ShapeDtypeStruct((2 * REF_ROWS, references.shape[2]), low),
            jax.ShapeDtypeStruct((CLASSES, img_dev), wide),
        ),
        in_specs=[far] * 6,
        out_specs=(vmem, vmem),
        scratch_shapes=[
            pltpu.VMEM(images.shape, wide),
            pltpu.VMEM(references.shape, wide),
            pltpu.VMEM((1, img_dev), wide),
            pltpu.VMEM((2, SHIFTS), jnp.int32),
            pltpu.VMEM((1, REF_ROWS), jnp.int32),
            pltpu.VMEM((1, CLASSES), wide),
            pltpu.VMEM((n_img, 2, img_dev, CHUNK), low),
            pltpu.VMEM((n_img, 2, img_dev, CHUNK), low),
            pltpu.VMEM((n_ref, 2 * REF_ROWS, CHUNK), low),
            pltpu.VMEM((n_ref, 2 * REF_ROWS, CHUNK), low),
            pltpu.VMEM((SHIFTS, 8, CHUNK), wide),
            pltpu.VMEM((SHIFTS, 8, CHUNK), wide),
            pltpu.VMEM((SHIFTS, n_images, 2 * CHUNK), low),
            pltpu.VMEM((SHIFTS, n_refs, 2 * CHUNK), low),
            pltpu.VMEM((n_refs, LANES), wide),
            pltpu.VMEM((CORES * per, 2 * REF_ROWS, CHUNK), low),
            pltpu.VMEM((strips, CORES * per, 2 * REF_ROWS, STRIP), low),
            pltpu.VMEM((GROUPS, n_img, img_dev, TOGETHER * n_refs), wide),
            pltpu.VMEM((GROUPS, n_img - 1, img_dev, TOGETHER * n_refs), wide),
            pltpu.VMEM((img_dev, 8, LANES), wide),
            pltpu.VMEM((n_ref - 1, OWNED, 8, LANES), wide),
            pltpu.VMEM((n_dev, 16, LANES), low),
            pltpu.VMEM((n_images, 8, LANES), wide),
            pltpu.VMEM((strips, n_ref, 2 * REF_ROWS, STRIP), low),
            pltpu.VMEM((strips, n_ref, 2 * REF_ROWS, STRIP), low),
        ]
        + [pltpu.SemaphoreType.DMA(count) for count in counts],
        compiler_params=pltpu.CompilerParams(
            collective_id=0, has_side_effects=True, vmem_limit_bytes=56 * 1024 * 1024
        ),
        cost_estimate=pl.CostEstimate(flops=800_000_000, bytes_accessed=2_000_000, transcendentals=25_000),
    )(
        images,
        references,
        precision.reshape(1, img_dev),
        shifts.T,
        labels.reshape(1, REF_ROWS),
        log_prior.reshape(1, CLASSES),
    )
    new_refs, class_rows = pl.pallas_call(
        widen_kernel,
        out_shape=(
            jax.ShapeDtypeStruct(references.shape, wide),
            jax.ShapeDtypeStruct((CLASSES, img_dev), wide),
        ),
        in_specs=[vmem, vmem],
        out_specs=(vmem, vmem),
        cost_estimate=pl.CostEstimate(flops=0, bytes_accessed=800_000, transcendentals=0),
    )(new_refs, class_rows)
    return new_refs, class_rows.T


def local(n_img, n_ref, images, references, precision, shifts, labels, log_prior):
    fits = (
        images.shape[1] == OWNED * n_ref
        and images.shape[1] % 16 == 0
        and references.shape[1] == REF_ROWS
        and 2 * n_ref * REF_ROWS == LANES
        and images.shape[2] == n_img * CHUNK
        and references.shape[2] == n_ref * CHUNK
        and n_ref % n_img == 0
        and n_img == 2 * CORES
    )
    if fits:
        return fused(n_img, n_ref, images, references, precision, shifts, labels, log_prior)
    return gathered(images, references, precision, shifts, labels, log_prior)


def solution(mesh):
    return jax.shard_map(
        functools.partial(local, mesh.shape["img"], mesh.shape["ref"]),
        mesh=mesh,
        in_specs=(P(None, "img", "ref"), P(None, "ref", "img"), P("img"), P(), P("ref"), P()),
        out_specs=(P(None, "ref", "img"), P("img", None)),
        check_vma=False,
    )
```

```python
import functools
import math

import jax
import jax.numpy as jnp
from jax import lax
from jax.experimental import pallas as pl
from jax.experimental.pallas import tpu as pltpu
from jax.sharding import PartitionSpec as P

ROWS = 256
COLS = 128
SHIFTS = 12
CLASSES = 4


def phases(shifts):
    index = jnp.arange(ROWS * COLS, dtype=jnp.int32)
    freq_y = (index // COLS - ROWS // 2).astype(jnp.float32)
    freq_x = (index % COLS).astype(jnp.float32)
    shift_x = shifts[:, 0].astype(jnp.float32)[:, None]
    shift_y = shifts[:, 1].astype(jnp.float32)[:, None]
    angles = 2.0 * math.pi / ROWS * (freq_x[None, :] * shift_x + freq_y[None, :] * shift_y)
    return (jnp.cos(angles), jnp.sin(angles))


def inner_rows(left, right):
    return lax.dot_general(
        left, right, (((1,), (1,)), ((), ())), preferred_element_type=jnp.float32
    )


def inner_cols(left, right):
    return lax.dot_general(
        left, right, (((0,), (0,)), ((), ())), preferred_element_type=jnp.float32
    )


def gathered(images, references, precision, shifts, labels, log_prior):
    img_low = lax.all_gather(images.astype(jnp.bfloat16), "ref", axis=2, tiled=True)
    ref_low = lax.all_gather(references.astype(jnp.bfloat16), "img", axis=2, tiled=True)
    pixels = img_low.shape[2]
    img_dev = img_low.shape[1]
    ref_dev = ref_low.shape[1]
    blocks = SHIFTS // 4
    cosine, sine_part = phases(shifts)
    cos_blocks = cosine.reshape(blocks, 4, pixels)
    sin_blocks = sine_part.reshape(blocks, 4, pixels)
    ref_wide = ref_low.astype(jnp.float32)
    energy = jnp.sum(ref_wide * ref_wide, axis=(0, 2))
    onehot = (labels[:, None] == jnp.arange(CLASSES, dtype=jnp.int32)[None, :]).astype(jnp.float32)
    prior_term = jnp.sum(onehot * log_prior[None, :], axis=1)

    def cross_block(operands):
        cos_rows, sin_rows = operands
        shifted_re = (
            ref_wide[0][None] * cos_rows[:, None, :] + ref_wide[1][None] * sin_rows[:, None, :]
        ).astype(jnp.bfloat16)
        shifted_im = (
            ref_wide[1][None] * cos_rows[:, None, :] - ref_wide[0][None] * sin_rows[:, None, :]
        ).astype(jnp.bfloat16)
        return inner_rows(img_low[0], shifted_re.reshape(4 * ref_dev, pixels)) + inner_rows(
            img_low[1], shifted_im.reshape(4 * ref_dev, pixels)
        )

    cross_terms = lax.map(cross_block, (cos_blocks, sin_blocks))
    cross_terms = jnp.transpose(cross_terms, (1, 0, 2)).reshape(img_dev, SHIFTS, ref_dev)
    scores = (
        precision[:, None, None] * (cross_terms - 0.5 * energy[None, None, :])
        + prior_term[None, None, :]
    )
    local_top = jnp.max(scores, axis=(1, 2))
    top_score = lax.pmax(local_top, "ref")
    exponent = jnp.exp(scores - top_score[:, None, None])
    local_class = jnp.einsum(
        "ik,kc->ic", jnp.sum(exponent, axis=1), onehot, precision=lax.Precision.HIGHEST
    )
    row_total, class_sum = lax.psum((jnp.sum(exponent, axis=(1, 2)), local_class), "ref")
    posterior = exponent / row_total[:, None, None]
    class_post = class_sum / row_total[:, None]
    local_mass = jnp.sum(posterior, axis=(0, 1))
    post_low = posterior.astype(jnp.bfloat16).reshape(img_dev, blocks, 4 * ref_dev)
    post_low = jnp.transpose(post_low, (1, 0, 2))

    def back_block(running, operands):
        weights_blk, cos_rows, sin_rows = operands
        back_re = inner_cols(weights_blk, img_low[0]).reshape(4, ref_dev, pixels)
        back_im = inner_cols(weights_blk, img_low[1]).reshape(4, ref_dev, pixels)
        part_re = jnp.sum(back_re * cos_rows[:, None, :] - back_im * sin_rows[:, None, :], axis=0)
        part_im = jnp.sum(back_im * cos_rows[:, None, :] + back_re * sin_rows[:, None, :], axis=0)
        return (running + jnp.stack([part_re, part_im]), None)

    start_sum = jnp.zeros((2, ref_dev, pixels), jnp.float32)
    summed, unused = lax.scan(back_block, start_sum, (post_low, cos_blocks, sin_blocks))
    summed_part = lax.psum_scatter(summed, "img", scatter_dimension=2, tiled=True)
    ref_mass = lax.psum(local_mass, "img")
    new_refs = summed_part / (ref_mass + 1.0)[None, :, None]
    return (new_refs, class_post)


MESH = pl.DeviceIdType.MESH
LANES = 128
CHUNK = 1024
OWNED = 2
PAIRS = SHIFTS // 2
TOGETHER = 4
GROUPS = SHIFTS // TOGETHER
STRIP = 512
CORES = 2
REF_ROWS = 8


def exchange(src, dst, send_sem, recv_sem, img, ref):
    return pltpu.make_async_remote_copy(
        src_ref=src, dst_ref=dst, send_sem=send_sem, recv_sem=recv_sem, device_id=(img, ref), device_id_type=MESH
    )


def fused_kernel(
    n_img, n_ref,
    images_hbm, references_hbm, precision_hbm, shifts_hbm, labels_hbm, log_prior_hbm,
    new_refs, class_post,
    images, references, precision, shifts, labels, log_prior,
    img_send, img_buf, ref_send, ref_buf, cos_tab, sin_tab, rotated, shifted,
    energy_col, ref_mid, part, part_in, own, own_in, post_buf, post_wide, out_send, out_buf, in_sem,
    img_ss, img_rs, ref_ss, ref_rs, part_ss, part_rs, own_ss, own_rs, post_ss, post_rs, out_ss, out_rs,
    ref_mid_ss, ref_mid_rs,
):
    n_dev = n_img * n_ref
    a = lax.axis_index("img")
    r = lax.axis_index("ref")
    me = a * n_ref + r
    per = n_ref // n_img
    img_dev = images.shape[1]
    n_images = n_img * img_dev
    n_refs = n_ref * REF_ROWS

    loads = [
        pltpu.make_async_copy(src, dst, in_sem.at[i])
        for i, (src, dst) in enumerate(
            (
                (references_hbm, references),
                (images_hbm, images),
                (shifts_hbm, shifts),
                (precision_hbm, precision),
                (labels_hbm, labels),
                (log_prior_hbm, log_prior),
            )
        )
    ]
    for load in loads:
        load.start()

    barrier = pltpu.get_barrier_semaphore()

    def greet(j, carry):
        other = lax.rem(me + j, n_dev)
        pl.semaphore_signal(barrier, inc=1, device_id=(other // n_ref, lax.rem(other, n_ref)), device_id_type=MESH)
        return carry

    lax.fori_loop(1, n_dev, greet, 0)

    loads[0].wait()
    for q in range(n_ref):
        px = pl.ds(q * CHUNK, CHUNK)
        both = jnp.concatenate([references[0, :, px], references[1, :, px]], axis=0)
        ref_send[q] = both.astype(jnp.bfloat16)

    pl.semaphore_wait(barrier, n_dev - 1)

    y, core = a // CORES, lax.rem(a, CORES)
    across = (1 - y) * CORES + core

    def ref_here(q):
        return (lax.rem(q, n_img) == a) & (per * a + q // n_img == r)

    def ref_by_way(q):
        at_mid = (lax.rem(q, n_img) == across) & (per * a + q // n_img == r)
        return (lax.rem(q, n_img) // CORES != y) & jnp.logical_not(at_mid)

    def ref_copy(q):
        return exchange(
            ref_send.at[q], ref_buf.at[r], ref_ss.at[q], ref_rs.at[r], lax.rem(q, n_img), per * a + q // n_img
        )

    def ref_hop(q):
        slot = (q // n_img) * CORES + lax.rem(q, CORES)
        return exchange(ref_send.at[q], ref_mid.at[slot], ref_ss.at[q], ref_mid_rs.at[slot], across, r)

    def hop_start(j, carry):
        q = lax.rem(me + j, n_ref)

        @pl.when(ref_by_way(q))
        def _():
            ref_hop(q).start()

        return carry

    lax.fori_loop(0, n_ref, hop_start, 0)

    def ref_start(j, carry):
        q = lax.rem(me + j, n_ref)
        here = ref_here(q)

        @pl.when(here)
        def _():
            ref_buf[r] = ref_send[q]

        @pl.when(jnp.logical_not(here | ref_by_way(q)))
        def _():
            ref_copy(q).start()

        return carry

    lax.fori_loop(0, n_ref, ref_start, 0)

    def ref_forward(slot):
        to_img = y * CORES + slot % CORES
        to_ref = per * across + slot // CORES
        return (to_img == a) & (to_ref == r), exchange(
            ref_mid.at[slot], ref_buf.at[r], ref_mid_ss.at[slot], ref_rs.at[r], to_img, to_ref
        )

    loads[1].wait()
    for q in range(n_img):
        img_send[q] = images[:, :, q * CHUNK : (q + 1) * CHUNK].astype(jnp.bfloat16)
    img_buf[a] = img_send[a]
    img_copies = []
    for j in range(1, n_img):
        dest = lax.rem(a + j, n_img)
        copy = exchange(img_send.at[dest], img_buf.at[a], img_ss.at[j], img_rs.at[j], dest, r)
        copy.start()
        img_copies.append(copy)

    for slot in range(per * CORES):
        stays, copy = ref_forward(slot)

        @pl.when(jnp.logical_not(stays))
        def _():
            exchange(ref_send.at[0], ref_mid.at[slot], ref_ss.at[0], ref_mid_rs.at[slot], across, r).wait_recv()
            copy.start()

    row_first = r * (n_img * CHUNK // COLS) + a * (CHUNK // COLS) - ROWS // 2
    freq_y = lax.broadcasted_iota(jnp.int32, (CHUNK // COLS, COLS), 0) + row_first
    freq_x = lax.broadcasted_iota(jnp.int32, (CHUNK // COLS, COLS), 1)

    for load in loads[2:]:
        load.wait()
    for t in range(SHIFTS):
        turn = freq_x * shifts[0:1, t : t + 1] + freq_y * shifts[1:2, t : t + 1]
        turn = ((turn + ROWS // 2) & (ROWS - 1)) - ROWS // 2
        angle = turn.astype(jnp.float32) * (2.0 * math.pi / ROWS)
        cosine = jnp.cos(angle)
        sine = jnp.sin(angle)
        for n in range(CHUNK // COLS):
            px = slice(n * COLS, (n + 1) * COLS)
            cos_tab[t, :, px] = jnp.broadcast_to(cosine[n : n + 1], (8, COLS))
            sin_tab[t, :, px] = jnp.broadcast_to(sine[n : n + 1], (8, COLS))

    row = lax.broadcasted_iota(jnp.int32, (8, LANES), 0)
    lane = lax.broadcasted_iota(jnp.int32, (8, LANES), 1)
    label_row = jnp.concatenate([labels[...].astype(jnp.float32)] * (LANES // REF_ROWS), axis=1)
    label_row = jnp.where((lane // REF_ROWS) % n_ref == r, jnp.broadcast_to(label_row, (8, LANES)), 0.0)

    def arrive(b):
        @pl.when(jnp.logical_not((a == r // per) & (b == r)))
        def _():
            exchange(ref_send.at[0], ref_buf.at[b], ref_ss.at[0], ref_rs.at[b], r // per, b).wait_recv()

    def shift(b, t):
        cos_row = cos_tab[t]
        sin_row = sin_tab[t]
        res = []
        ims = []
        for s in range(2):
            block = ref_buf[b + s].astype(jnp.float32)
            re = block[0:REF_ROWS]
            im = block[REF_ROWS : 2 * REF_ROWS]
            res.append(re * cos_row + im * sin_row)
            ims.append(im * cos_row - re * sin_row)
        rows = pl.ds(pl.multiple_of(b * REF_ROWS, 2 * REF_ROWS), 2 * REF_ROWS)
        shifted[t, rows, 0:CHUNK] = jnp.concatenate(res, axis=0).astype(jnp.bfloat16)
        shifted[t, rows, CHUNK : 2 * CHUNK] = jnp.concatenate(ims, axis=0).astype(jnp.bfloat16)

    def ready(b):
        arrive(b)
        arrive(b + 1)
        for s in range(2):
            block = ref_buf[b + s].astype(jnp.float32)
            square = jnp.sum(block * block, axis=1, keepdims=True)
            square = jnp.broadcast_to(square[0:REF_ROWS] + square[REF_ROWS : 2 * REF_ROWS], (REF_ROWS, LANES))
            energy_col[pl.ds(pl.multiple_of((b + s) * REF_ROWS, REF_ROWS), REF_ROWS)] = square

    layers = n_ref // 2

    def layer_step(i, carry):
        b = 2 * lax.rem(r // 2 + i, layers)
        ready(b)

        def turn_step(t, inner):
            shift(b, t)
            return inner

        return lax.fori_loop(0, SHIFTS, turn_step, carry)

    lax.fori_loop(0, layers - 1, layer_step, 0)
    last = 2 * lax.rem(r // 2 + layers - 1, layers)
    ready(last)
    energy = energy_col[...]
    half_energy = 0.5 * jnp.concatenate([energy, energy], axis=0).T[0:8][None]

    for copy in img_copies:
        copy.wait_recv()

    def rotate(t, carry):
        cos_row = cos_tab[t][None]
        sin_row = sin_tab[t][None]
        for b in range(n_img):
            re = img_buf[b, 0].astype(jnp.float32).reshape(img_dev // 8, 8, CHUNK)
            im = img_buf[b, 1].astype(jnp.float32).reshape(img_dev // 8, 8, CHUNK)
            rows = pl.ds(b * img_dev, img_dev)
            turned_re = (re * cos_row - im * sin_row).reshape(img_dev, CHUNK)
            turned_im = (im * cos_row + re * sin_row).reshape(img_dev, CHUNK)
            rotated[t, rows, 0:CHUNK] = turned_re.astype(jnp.bfloat16)
            rotated[t, rows, CHUNK : 2 * CHUNK] = turned_im.astype(jnp.bfloat16)
        return carry

    pictures = [img_buf[:, c].reshape(n_images, CHUNK) for c in range(2)]
    pictures = jnp.concatenate(pictures, axis=1)
    part_copies = []
    for g in range(GROUPS):
        for t in range(g * TOGETHER, (g + 1) * TOGETHER):
            shift(last, t)
        group = shifted[g * TOGETHER : (g + 1) * TOGETHER].reshape(TOGETHER * n_refs, 2 * CHUNK)
        cross = inner_rows(pictures, group)
        for h in range(TOGETHER // 2):
            pair = cross[:, h * LANES : (h + 1) * LANES]
            pair = (pair.reshape(n_images // 8, 8, LANES) - half_energy).reshape(n_img, img_dev, LANES)
            part[g, :, :, h * LANES : (h + 1) * LANES] = pair
        for j in range(1, n_img):
            dest = lax.rem(a + j, n_img)
            copy = exchange(
                part.at[g, dest], part_in.at[g, j - 1], part_ss.at[g, j], part_rs.at[g, j], dest, r
            )
            copy.start()
            part_copies.append(copy)

    own[...] = jnp.zeros_like(own)
    own[:, PAIRS, :] = jnp.broadcast_to(label_row[0:1], (img_dev, LANES))
    lax.fori_loop(0, TOGETHER, rotate, 0)
    for copy in part_copies:
        copy.wait_recv()
    for g in range(GROUPS):
        total = part[g, a]
        for j in range(n_img - 1):
            total = total + part_in[g, j]
        for h in range(TOGETHER // 2):
            own[:, g * (TOGETHER // 2) + h, :] = total[:, h * LANES : (h + 1) * LANES]
    own_copies = []
    for j in range(1, n_ref):
        dest = lax.rem(r + j, n_ref)
        copy = exchange(own.at[pl.ds(OWNED * dest, OWNED)], own_in.at[j - 1], own_ss.at[j], own_rs.at[j], a, dest)
        copy.start()
        own_copies.append(copy)
    lax.fori_loop(TOGETHER, 2 * TOGETHER, rotate, 0)
    for copy in own_copies:
        copy.wait_recv()
    mine = own[pl.ds(OWNED * r, OWNED)]
    for j in range(n_ref - 1):
        mine = mine + own_in[j]
    label_lane = jnp.broadcast_to(mine[0, PAIRS : PAIRS + 1], (8, LANES))
    prior = jnp.zeros((8, LANES), jnp.float32)
    for c in range(CLASSES):
        prior = prior + jnp.where(label_lane == c, log_prior[:, c : c + 1], 0.0)
    image_lane = lax.broadcasted_iota(jnp.int32, (1, img_dev), 1)

    blocks = []
    for il in range(OWNED):
        noise = jnp.sum(jnp.where(image_lane == OWNED * r + il, precision[...], 0.0), axis=1, keepdims=True)
        scores = noise * mine[il] + prior
        scores = jnp.where(row < PAIRS, scores, -jnp.inf)
        top = jnp.max(jnp.max(scores, axis=1, keepdims=True), axis=0, keepdims=True)
        exponent = jnp.exp(scores - top)
        row_total = jnp.sum(jnp.sum(exponent, axis=1, keepdims=True), axis=0, keepdims=True)
        posterior = exponent / row_total
        lane_sum = jnp.broadcast_to(jnp.sum(posterior, axis=0, keepdims=True), (8, LANES))
        totals = lane_sum + pltpu.roll(lane_sum, n_refs, 1)
        for c in range(CLASSES):
            in_class = jnp.sum(jnp.where(label_lane == c, lane_sum, 0.0), axis=1, keepdims=True)
            totals = jnp.where(lane == n_refs + c, in_class, totals)
        high = totals.astype(jnp.bfloat16).astype(jnp.float32)
        block = jnp.where(row == PAIRS, high, posterior)
        blocks.append(jnp.where(row == PAIRS + 1, totals - high, block))
    post_buf[me] = jnp.concatenate(blocks, axis=0).astype(jnp.bfloat16)

    def post_copy(j):
        other = lax.rem(me + j, n_dev)
        return exchange(
            post_buf.at[me], post_buf.at[me], post_ss.at[j], post_rs.at[j], other // n_ref, lax.rem(other, n_ref)
        )

    def post_start(j, carry):
        post_copy(j).start()
        return carry

    lax.fori_loop(1, n_dev, post_start, 0)

    lax.fori_loop(2 * TOGETHER, SHIFTS, rotate, 0)

    def post_arrive(j, carry):
        source = lax.rem(me + n_dev - j, n_dev)
        exchange(
            post_buf.at[me], post_buf.at[source], post_ss.at[j], post_rs.at[j], source // n_ref, lax.rem(source, n_ref)
        ).wait_recv()
        return carry

    lax.fori_loop(1, n_dev, post_arrive, 0)

    post_wide[...] = post_buf[...].astype(jnp.float32).reshape(n_images, 8, LANES)
    totals = post_wide[:, PAIRS, :] + post_wide[:, PAIRS + 1, :]
    mass = jnp.broadcast_to(jnp.sum(totals, axis=0, keepdims=True), (LANES, LANES)).T[0:n_refs]
    scale = 1.0 / (mass[:, 0:1] + 1.0)
    first = pl.ds(a * img_dev, img_dev)
    mine = post_wide[first, PAIRS, :] + post_wide[first, PAIRS + 1, :]
    class_post[...] = jnp.concatenate([mine] * (LANES // img_dev), axis=0).T[n_refs : n_refs + CLASSES, 0:img_dev]
    weights = []
    for tp in range(PAIRS):
        both = post_wide[:, tp, :].T
        weights.append(jnp.concatenate([both[0:n_refs], both[n_refs : 2 * n_refs]], axis=1).astype(jnp.bfloat16))
    weights = jnp.concatenate(weights, axis=1)
    turned = rotated[...].reshape(SHIFTS * n_images, 2 * CHUNK)
    piece = lax.rem(r, per) * n_img + a

    target = r // per

    def out_copy(h, j):
        return exchange(
            out_send.at[h, j], out_buf.at[h, piece], out_ss.at[h, j], out_rs.at[h, piece], target, j
        )

    for h in range(CHUNK // STRIP):
        real = jnp.dot(weights, turned[:, h * STRIP : (h + 1) * STRIP], preferred_element_type=jnp.float32)
        imag = jnp.dot(
            weights, turned[:, CHUNK + h * STRIP : CHUNK + (h + 1) * STRIP], preferred_element_type=jnp.float32
        )
        real = (real * scale).reshape(n_ref, REF_ROWS, STRIP)
        imag = (imag * scale).reshape(n_ref, REF_ROWS, STRIP)
        out_send[h] = jnp.concatenate([real, imag], axis=1).astype(jnp.bfloat16)

        def out_start(i, carry):
            j = lax.rem(r + i, n_ref)
            here = (a == target) & (j == r)

            @pl.when(here)
            def _():
                out_buf[h, piece] = out_send[h, j]

            @pl.when(jnp.logical_not(here))
            def _():
                out_copy(h, j).start()

            return carry

        lax.fori_loop(0, n_ref, out_start, 0)

    for copy in img_copies + part_copies + own_copies:
        copy.wait_send()

    def post_sent(j, carry):
        post_copy(j).wait_send()
        return carry

    lax.fori_loop(1, n_dev, post_sent, 0)

    def ref_sent(j, carry):
        @pl.when(jnp.logical_not(ref_here(j)))
        def _():
            ref_copy(j).wait_send()

        return carry

    lax.fori_loop(0, n_ref, ref_sent, 0)
    for slot in range(per * CORES):
        stays, copy = ref_forward(slot)

        @pl.when(jnp.logical_not(stays))
        def _():
            copy.wait_send()

    for h in range(CHUNK // STRIP):
        for q in range(n_ref):
            @pl.when(jnp.logical_not(ref_here(q)))
            def _():
                exchange(
                    out_send.at[h, 0], out_buf.at[h, q], out_ss.at[h, 0], out_rs.at[h, q],
                    q % n_img, per * a + q // n_img,
                ).wait_recv()

            new_refs[:, q * CHUNK + h * STRIP : q * CHUNK + (h + 1) * STRIP] = out_buf[h, q]

    def out_sent(j, carry):
        @pl.when(jnp.logical_not((a == target) & (j == r)))
        def _():
            for h in range(CHUNK // STRIP):
                out_copy(h, j).wait_send()

        return carry

    lax.fori_loop(0, n_ref, out_sent, 0)


def widen_kernel(low, class_rows, new_refs, class_post):
    for q in range(low.shape[1] // CHUNK):
        px = slice(q * CHUNK, (q + 1) * CHUNK)
        block = low[:, px].astype(jnp.float32)
        new_refs[0, :, px] = block[0:REF_ROWS]
        new_refs[1, :, px] = block[REF_ROWS : 2 * REF_ROWS]
    class_post[...] = class_rows[...]


def fused(n_img, n_ref, images, references, precision, shifts, labels, log_prior):
    img_dev = images.shape[1]
    n_images = n_img * img_dev
    n_refs = n_ref * REF_ROWS
    n_dev = n_img * n_ref
    vmem = pl.BlockSpec(memory_space=pltpu.VMEM)
    far = pl.BlockSpec(memory_space=pl.ANY)
    low = jnp.bfloat16
    wide = jnp.float32
    strips = CHUNK // STRIP
    per = n_ref // n_img
    parts = (GROUPS, n_img)
    outs = (strips, n_ref)
    counts = ((6,), (n_img,), (n_img,), (n_ref,), (n_ref,), parts, parts)
    counts = counts + ((n_ref,), (n_ref,), (n_dev,), (n_dev,), outs, outs)
    counts = counts + ((CORES * per,), (CORES * per,))
    new_refs, class_rows = pl.pallas_call(
        functools.partial(fused_kernel, n_img, n_ref),
        out_shape=(
            jax.ShapeDtypeStruct((2 * REF_ROWS, references.shape[2]), low),
            jax.ShapeDtypeStruct((CLASSES, img_dev), wide),
        ),
        in_specs=[far] * 6,
        out_specs=(vmem, vmem),
        scratch_shapes=[
            pltpu.VMEM(images.shape, wide),
            pltpu.VMEM(references.shape, wide),
            pltpu.VMEM((1, img_dev), wide),
            pltpu.VMEM((2, SHIFTS), jnp.int32),
            pltpu.VMEM((1, REF_ROWS), jnp.int32),
            pltpu.VMEM((1, CLASSES), wide),
            pltpu.VMEM((n_img, 2, img_dev, CHUNK), low),
            pltpu.VMEM((n_img, 2, img_dev, CHUNK), low),
            pltpu.VMEM((n_ref, 2 * REF_ROWS, CHUNK), low),
            pltpu.VMEM((n_ref, 2 * REF_ROWS, CHUNK), low),
            pltpu.VMEM((SHIFTS, 8, CHUNK), wide),
            pltpu.VMEM((SHIFTS, 8, CHUNK), wide),
            pltpu.VMEM((SHIFTS, n_images, 2 * CHUNK), low),
            pltpu.VMEM((SHIFTS, n_refs, 2 * CHUNK), low),
            pltpu.VMEM((n_refs, LANES), wide),
            pltpu.VMEM((CORES * per, 2 * REF_ROWS, CHUNK), low),
            pltpu.VMEM((GROUPS, n_img, img_dev, TOGETHER * n_refs), wide),
            pltpu.VMEM((GROUPS, n_img - 1, img_dev, TOGETHER * n_refs), wide),
            pltpu.VMEM((img_dev, 8, LANES), wide),
            pltpu.VMEM((n_ref - 1, OWNED, 8, LANES), wide),
            pltpu.VMEM((n_dev, 16, LANES), low),
            pltpu.VMEM((n_images, 8, LANES), wide),
            pltpu.VMEM((strips, n_ref, 2 * REF_ROWS, STRIP), low),
            pltpu.VMEM((strips, n_ref, 2 * REF_ROWS, STRIP), low),
        ]
        + [pltpu.SemaphoreType.DMA(count) for count in counts],
        compiler_params=pltpu.CompilerParams(
            collective_id=0, has_side_effects=True, vmem_limit_bytes=56 * 1024 * 1024
        ),
        cost_estimate=pl.CostEstimate(flops=800_000_000, bytes_accessed=2_000_000, transcendentals=25_000),
    )(
        images,
        references,
        precision.reshape(1, img_dev),
        shifts.T,
        labels.reshape(1, REF_ROWS),
        log_prior.reshape(1, CLASSES),
    )
    new_refs, class_rows = pl.pallas_call(
        widen_kernel,
        out_shape=(
            jax.ShapeDtypeStruct(references.shape, wide),
            jax.ShapeDtypeStruct((CLASSES, img_dev), wide),
        ),
        in_specs=[vmem, vmem],
        out_specs=(vmem, vmem),
        cost_estimate=pl.CostEstimate(flops=0, bytes_accessed=800_000, transcendentals=0),
    )(new_refs, class_rows)
    return new_refs, class_rows.T


def local(n_img, n_ref, images, references, precision, shifts, labels, log_prior):
    fits = (
        images.shape[1] == OWNED * n_ref
        and images.shape[1] % 16 == 0
        and references.shape[1] == REF_ROWS
        and 2 * n_ref * REF_ROWS == LANES
        and images.shape[2] == n_img * CHUNK
        and references.shape[2] == n_ref * CHUNK
        and n_ref % n_img == 0
        and n_img == 2 * CORES
    )
    if fits:
        return fused(n_img, n_ref, images, references, precision, shifts, labels, log_prior)
    return gathered(images, references, precision, shifts, labels, log_prior)


def solution(mesh):
    return jax.shard_map(
        functools.partial(local, mesh.shape["img"], mesh.shape["ref"]),
        mesh=mesh,
        in_specs=(P(None, "img", "ref"), P(None, "ref", "img"), P("img"), P(), P("ref"), P()),
        out_specs=(P(None, "ref", "img"), P("img", None)),
        check_vma=False,
    )
```

```python
import functools
import math

import jax
import jax.numpy as jnp
from jax import lax
from jax.experimental import pallas as pl
from jax.experimental.pallas import tpu as pltpu
from jax.sharding import PartitionSpec as P

ROWS = 256
COLS = 128
SHIFTS = 12
CLASSES = 4


def phases(shifts):
    index = jnp.arange(ROWS * COLS, dtype=jnp.int32)
    freq_y = (index // COLS - ROWS // 2).astype(jnp.float32)
    freq_x = (index % COLS).astype(jnp.float32)
    shift_x = shifts[:, 0].astype(jnp.float32)[:, None]
    shift_y = shifts[:, 1].astype(jnp.float32)[:, None]
    angles = 2.0 * math.pi / ROWS * (freq_x[None, :] * shift_x + freq_y[None, :] * shift_y)
    return (jnp.cos(angles), jnp.sin(angles))


def inner_rows(left, right):
    return lax.dot_general(
        left, right, (((1,), (1,)), ((), ())), preferred_element_type=jnp.float32
    )


def inner_cols(left, right):
    return lax.dot_general(
        left, right, (((0,), (0,)), ((), ())), preferred_element_type=jnp.float32
    )


def gathered(images, references, precision, shifts, labels, log_prior):
    img_low = lax.all_gather(images.astype(jnp.bfloat16), "ref", axis=2, tiled=True)
    ref_low = lax.all_gather(references.astype(jnp.bfloat16), "img", axis=2, tiled=True)
    pixels = img_low.shape[2]
    img_dev = img_low.shape[1]
    ref_dev = ref_low.shape[1]
    blocks = SHIFTS // 4
    cosine, sine_part = phases(shifts)
    cos_blocks = cosine.reshape(blocks, 4, pixels)
    sin_blocks = sine_part.reshape(blocks, 4, pixels)
    ref_wide = ref_low.astype(jnp.float32)
    energy = jnp.sum(ref_wide * ref_wide, axis=(0, 2))
    onehot = (labels[:, None] == jnp.arange(CLASSES, dtype=jnp.int32)[None, :]).astype(jnp.float32)
    prior_term = jnp.sum(onehot * log_prior[None, :], axis=1)

    def cross_block(operands):
        cos_rows, sin_rows = operands
        shifted_re = (
            ref_wide[0][None] * cos_rows[:, None, :] + ref_wide[1][None] * sin_rows[:, None, :]
        ).astype(jnp.bfloat16)
        shifted_im = (
            ref_wide[1][None] * cos_rows[:, None, :] - ref_wide[0][None] * sin_rows[:, None, :]
        ).astype(jnp.bfloat16)
        return inner_rows(img_low[0], shifted_re.reshape(4 * ref_dev, pixels)) + inner_rows(
            img_low[1], shifted_im.reshape(4 * ref_dev, pixels)
        )

    cross_terms = lax.map(cross_block, (cos_blocks, sin_blocks))
    cross_terms = jnp.transpose(cross_terms, (1, 0, 2)).reshape(img_dev, SHIFTS, ref_dev)
    scores = (
        precision[:, None, None] * (cross_terms - 0.5 * energy[None, None, :])
        + prior_term[None, None, :]
    )
    local_top = jnp.max(scores, axis=(1, 2))
    top_score = lax.pmax(local_top, "ref")
    exponent = jnp.exp(scores - top_score[:, None, None])
    local_class = jnp.einsum(
        "ik,kc->ic", jnp.sum(exponent, axis=1), onehot, precision=lax.Precision.HIGHEST
    )
    row_total, class_sum = lax.psum((jnp.sum(exponent, axis=(1, 2)), local_class), "ref")
    posterior = exponent / row_total[:, None, None]
    class_post = class_sum / row_total[:, None]
    local_mass = jnp.sum(posterior, axis=(0, 1))
    post_low = posterior.astype(jnp.bfloat16).reshape(img_dev, blocks, 4 * ref_dev)
    post_low = jnp.transpose(post_low, (1, 0, 2))

    def back_block(running, operands):
        weights_blk, cos_rows, sin_rows = operands
        back_re = inner_cols(weights_blk, img_low[0]).reshape(4, ref_dev, pixels)
        back_im = inner_cols(weights_blk, img_low[1]).reshape(4, ref_dev, pixels)
        part_re = jnp.sum(back_re * cos_rows[:, None, :] - back_im * sin_rows[:, None, :], axis=0)
        part_im = jnp.sum(back_im * cos_rows[:, None, :] + back_re * sin_rows[:, None, :], axis=0)
        return (running + jnp.stack([part_re, part_im]), None)

    start_sum = jnp.zeros((2, ref_dev, pixels), jnp.float32)
    summed, unused = lax.scan(back_block, start_sum, (post_low, cos_blocks, sin_blocks))
    summed_part = lax.psum_scatter(summed, "img", scatter_dimension=2, tiled=True)
    ref_mass = lax.psum(local_mass, "img")
    new_refs = summed_part / (ref_mass + 1.0)[None, :, None]
    return (new_refs, class_post)


MESH = pl.DeviceIdType.MESH
LANES = 128
CHUNK = 1024
OWNED = 2
PAIRS = SHIFTS // 2
TOGETHER = 4
GROUPS = SHIFTS // TOGETHER
STRIP = 512
CORES = 2
REF_ROWS = 8


def exchange(src, dst, send_sem, recv_sem, img, ref):
    return pltpu.make_async_remote_copy(
        src_ref=src, dst_ref=dst, send_sem=send_sem, recv_sem=recv_sem, device_id=(img, ref), device_id_type=MESH
    )


def fused_kernel(
    n_img, n_ref,
    images_hbm, references_hbm, precision_hbm, shifts_hbm, labels_hbm, log_prior_hbm,
    new_refs, class_post,
    images, references, precision, shifts, labels, log_prior,
    img_send, img_buf, ref_send, ref_buf, cos_tab, sin_tab, rotated, shifted,
    energy_col, ref_mid, part, part_in, own, own_in, post_buf, post_wide, out_send, out_buf, in_sem,
    img_ss, img_rs, ref_ss, ref_rs, part_ss, part_rs, own_ss, own_rs, post_ss, post_rs, out_ss, out_rs,
    ref_mid_ss, ref_mid_rs,
):
    n_dev = n_img * n_ref
    a = lax.axis_index("img")
    r = lax.axis_index("ref")
    me = a * n_ref + r
    per = n_ref // n_img
    img_dev = images.shape[1]
    n_images = n_img * img_dev
    n_refs = n_ref * REF_ROWS

    loads = [
        pltpu.make_async_copy(src, dst, in_sem.at[i])
        for i, (src, dst) in enumerate(
            (
                (references_hbm, references),
                (images_hbm, images),
                (shifts_hbm, shifts),
                (precision_hbm, precision),
                (labels_hbm, labels),
                (log_prior_hbm, log_prior),
            )
        )
    ]
    for load in loads:
        load.start()

    barrier = pltpu.get_barrier_semaphore()

    def greet(j, carry):
        other = lax.rem(me + j, n_dev)
        pl.semaphore_signal(barrier, inc=1, device_id=(other // n_ref, lax.rem(other, n_ref)), device_id_type=MESH)
        return carry

    lax.fori_loop(1, n_dev, greet, 0)

    loads[0].wait()
    for q in range(n_ref):
        px = pl.ds(q * CHUNK, CHUNK)
        both = jnp.concatenate([references[0, :, px], references[1, :, px]], axis=0)
        ref_send[q] = both.astype(jnp.bfloat16)

    pl.semaphore_wait(barrier, n_dev - 1)

    y, core = a // CORES, lax.rem(a, CORES)
    across = (1 - y) * CORES + core

    def ref_here(q):
        return (lax.rem(q, n_img) == a) & (per * a + q // n_img == r)

    def ref_by_way(q):
        at_mid = (lax.rem(q, n_img) == across) & (per * a + q // n_img == r)
        return (lax.rem(q, n_img) // CORES != y) & jnp.logical_not(at_mid)

    def ref_copy(q):
        return exchange(
            ref_send.at[q], ref_buf.at[r], ref_ss.at[q], ref_rs.at[r], lax.rem(q, n_img), per * a + q // n_img
        )

    def ref_hop(q):
        slot = (q // n_img) * CORES + lax.rem(q, CORES)
        return exchange(ref_send.at[q], ref_mid.at[slot], ref_ss.at[q], ref_mid_rs.at[slot], across, r)

    def hop_start(j, carry):
        q = lax.rem(me + j, n_ref)

        @pl.when(ref_by_way(q))
        def _():
            ref_hop(q).start()

        return carry

    lax.fori_loop(0, n_ref, hop_start, 0)

    def ref_start(j, carry):
        q = lax.rem(me + j, n_ref)
        here = ref_here(q)

        @pl.when(here)
        def _():
            ref_buf[r] = ref_send[q]

        @pl.when(jnp.logical_not(here | ref_by_way(q)))
        def _():
            ref_copy(q).start()

        return carry

    lax.fori_loop(0, n_ref, ref_start, 0)

    def ref_forward(slot):
        to_img = y * CORES + slot % CORES
        to_ref = per * across + slot // CORES
        return (to_img == a) & (to_ref == r), exchange(
            ref_mid.at[slot], ref_buf.at[r], ref_mid_ss.at[slot], ref_rs.at[r], to_img, to_ref
        )

    loads[1].wait()
    for q in range(n_img):
        img_send[q] = images[:, :, q * CHUNK : (q + 1) * CHUNK].astype(jnp.bfloat16)
    img_buf[a] = img_send[a]
    img_copies = []
    for j in range(1, n_img):
        dest = lax.rem(a + j, n_img)
        copy = exchange(img_send.at[dest], img_buf.at[a], img_ss.at[j], img_rs.at[j], dest, r)
        copy.start()
        img_copies.append(copy)

    for slot in range(per * CORES):
        stays, copy = ref_forward(slot)

        @pl.when(jnp.logical_not(stays))
        def _():
            exchange(ref_send.at[0], ref_mid.at[slot], ref_ss.at[0], ref_mid_rs.at[slot], across, r).wait_recv()
            copy.start()

    row_first = r * (n_img * CHUNK // COLS) + a * (CHUNK // COLS) - ROWS // 2
    freq_y = lax.broadcasted_iota(jnp.int32, (CHUNK // COLS, COLS), 0) + row_first
    freq_x = lax.broadcasted_iota(jnp.int32, (CHUNK // COLS, COLS), 1)

    for load in loads[2:]:
        load.wait()
    for t in range(SHIFTS):
        turn = freq_x * shifts[0:1, t : t + 1] + freq_y * shifts[1:2, t : t + 1]
        turn = ((turn + ROWS // 2) & (ROWS - 1)) - ROWS // 2
        angle = turn.astype(jnp.float32) * (2.0 * math.pi / ROWS)
        cosine = jnp.cos(angle)
        sine = jnp.sin(angle)
        for n in range(CHUNK // COLS):
            px = slice(n * COLS, (n + 1) * COLS)
            cos_tab[t, :, px] = jnp.broadcast_to(cosine[n : n + 1], (8, COLS))
            sin_tab[t, :, px] = jnp.broadcast_to(sine[n : n + 1], (8, COLS))

    row = lax.broadcasted_iota(jnp.int32, (8, LANES), 0)
    lane = lax.broadcasted_iota(jnp.int32, (8, LANES), 1)
    label_row = jnp.concatenate([labels[...].astype(jnp.float32)] * (LANES // REF_ROWS), axis=1)
    label_row = jnp.where((lane // REF_ROWS) % n_ref == r, jnp.broadcast_to(label_row, (8, LANES)), 0.0)

    def arrive(b):
        @pl.when(jnp.logical_not((a == r // per) & (b == r)))
        def _():
            exchange(ref_send.at[0], ref_buf.at[b], ref_ss.at[0], ref_rs.at[b], r // per, b).wait_recv()

    def shift(b, t):
        cos_row = cos_tab[t]
        sin_row = sin_tab[t]
        res = []
        ims = []
        for s in range(2):
            block = ref_buf[b + s].astype(jnp.float32)
            re = block[0:REF_ROWS]
            im = block[REF_ROWS : 2 * REF_ROWS]
            res.append(re * cos_row + im * sin_row)
            ims.append(im * cos_row - re * sin_row)
        rows = pl.ds(pl.multiple_of(b * REF_ROWS, 2 * REF_ROWS), 2 * REF_ROWS)
        shifted[t, rows, 0:CHUNK] = jnp.concatenate(res, axis=0).astype(jnp.bfloat16)
        shifted[t, rows, CHUNK : 2 * CHUNK] = jnp.concatenate(ims, axis=0).astype(jnp.bfloat16)

    def ready(b):
        arrive(b)
        arrive(b + 1)
        for s in range(2):
            block = ref_buf[b + s].astype(jnp.float32)
            square = jnp.sum(block * block, axis=1, keepdims=True)
            square = jnp.broadcast_to(square[0:REF_ROWS] + square[REF_ROWS : 2 * REF_ROWS], (REF_ROWS, LANES))
            energy_col[pl.ds(pl.multiple_of((b + s) * REF_ROWS, REF_ROWS), REF_ROWS)] = square

    layers = n_ref // 2

    def layer_step(i, carry):
        b = 2 * lax.rem(r // 2 + i, layers)
        ready(b)

        def turn_step(t, inner):
            shift(b, t)
            return inner

        return lax.fori_loop(0, SHIFTS, turn_step, carry)

    lax.fori_loop(0, layers - 1, layer_step, 0)
    last = 2 * lax.rem(r // 2 + layers - 1, layers)
    ready(last)
    energy = energy_col[...]
    half_energy = 0.5 * jnp.concatenate([energy, energy], axis=0).T[0:8][None]

    for copy in img_copies:
        copy.wait_recv()

    def rotate(t, carry):
        cos_row = cos_tab[t][None]
        sin_row = sin_tab[t][None]
        for b in range(n_img):
            re = img_buf[b, 0].astype(jnp.float32).reshape(img_dev // 8, 8, CHUNK)
            im = img_buf[b, 1].astype(jnp.float32).reshape(img_dev // 8, 8, CHUNK)
            rows = pl.ds(b * img_dev, img_dev)
            turned_re = (re * cos_row - im * sin_row).reshape(img_dev, CHUNK)
            turned_im = (im * cos_row + re * sin_row).reshape(img_dev, CHUNK)
            rotated[t, rows, 0:CHUNK] = turned_re.astype(jnp.bfloat16)
            rotated[t, rows, CHUNK : 2 * CHUNK] = turned_im.astype(jnp.bfloat16)
        return carry

    pictures = [img_buf[:, c].reshape(n_images, CHUNK) for c in range(2)]
    pictures = jnp.concatenate(pictures, axis=1)
    pictures = jnp.concatenate([pictures] * (LANES // n_images), axis=0)
    part_copies = []
    for g in range(GROUPS):
        for t in range(g * TOGETHER, (g + 1) * TOGETHER):
            shift(last, t)
        group = shifted[g * TOGETHER : (g + 1) * TOGETHER].reshape(TOGETHER * n_refs, 2 * CHUNK)
        cross = inner_rows(group, pictures).T[0:n_images]
        for h in range(TOGETHER // 2):
            pair = cross[:, h * LANES : (h + 1) * LANES]
            pair = (pair.reshape(n_images // 8, 8, LANES) - half_energy).reshape(n_img, img_dev, LANES)
            part[g, :, :, h * LANES : (h + 1) * LANES] = pair
        for j in range(1, n_img):
            dest = lax.rem(a + j, n_img)
            copy = exchange(
                part.at[g, dest], part_in.at[g, j - 1], part_ss.at[g, j], part_rs.at[g, j], dest, r
            )
            copy.start()
            part_copies.append(copy)

    own[...] = jnp.zeros_like(own)
    own[:, PAIRS, :] = jnp.broadcast_to(label_row[0:1], (img_dev, LANES))
    lax.fori_loop(0, TOGETHER, rotate, 0)
    for copy in part_copies:
        copy.wait_recv()
    for g in range(GROUPS):
        total = part[g, a]
        for j in range(n_img - 1):
            total = total + part_in[g, j]
        for h in range(TOGETHER // 2):
            own[:, g * (TOGETHER // 2) + h, :] = total[:, h * LANES : (h + 1) * LANES]
    own_copies = []
    for j in range(1, n_ref):
        dest = lax.rem(r + j, n_ref)
        copy = exchange(own.at[pl.ds(OWNED * dest, OWNED)], own_in.at[j - 1], own_ss.at[j], own_rs.at[j], a, dest)
        copy.start()
        own_copies.append(copy)
    lax.fori_loop(TOGETHER, 2 * TOGETHER, rotate, 0)
    for copy in own_copies:
        copy.wait_recv()
    mine = own[pl.ds(OWNED * r, OWNED)]
    for j in range(n_ref - 1):
        mine = mine + own_in[j]
    label_lane = jnp.broadcast_to(mine[0, PAIRS : PAIRS + 1], (8, LANES))
    prior = jnp.zeros((8, LANES), jnp.float32)
    for c in range(CLASSES):
        prior = prior + jnp.where(label_lane == c, log_prior[:, c : c + 1], 0.0)
    image_lane = lax.broadcasted_iota(jnp.int32, (1, img_dev), 1)

    blocks = []
    for il in range(OWNED):
        noise = jnp.sum(jnp.where(image_lane == OWNED * r + il, precision[...], 0.0), axis=1, keepdims=True)
        scores = noise * mine[il] + prior
        scores = jnp.where(row < PAIRS, scores, -jnp.inf)
        top = jnp.max(jnp.max(scores, axis=1, keepdims=True), axis=0, keepdims=True)
        exponent = jnp.exp(scores - top)
        row_total = jnp.sum(jnp.sum(exponent, axis=1, keepdims=True), axis=0, keepdims=True)
        posterior = exponent / row_total
        lane_sum = jnp.broadcast_to(jnp.sum(posterior, axis=0, keepdims=True), (8, LANES))
        totals = lane_sum + pltpu.roll(lane_sum, n_refs, 1)
        for c in range(CLASSES):
            in_class = jnp.sum(jnp.where(label_lane == c, lane_sum, 0.0), axis=1, keepdims=True)
            totals = jnp.where(lane == n_refs + c, in_class, totals)
        high = totals.astype(jnp.bfloat16).astype(jnp.float32)
        block = jnp.where(row == PAIRS, high, posterior)
        blocks.append(jnp.where(row == PAIRS + 1, totals - high, block))
    post_buf[me] = jnp.concatenate(blocks, axis=0).astype(jnp.bfloat16)

    def post_copy(j):
        other = lax.rem(me + j, n_dev)
        return exchange(
            post_buf.at[me], post_buf.at[me], post_ss.at[j], post_rs.at[j], other // n_ref, lax.rem(other, n_ref)
        )

    def post_start(j, carry):
        post_copy(j).start()
        return carry

    lax.fori_loop(1, n_dev, post_start, 0)

    lax.fori_loop(2 * TOGETHER, SHIFTS, rotate, 0)

    def post_arrive(j, carry):
        source = lax.rem(me + n_dev - j, n_dev)
        exchange(
            post_buf.at[me], post_buf.at[source], post_ss.at[j], post_rs.at[j], source // n_ref, lax.rem(source, n_ref)
        ).wait_recv()
        return carry

    lax.fori_loop(1, n_dev, post_arrive, 0)

    post_wide[...] = post_buf[...].astype(jnp.float32).reshape(n_images, 8, LANES)
    totals = post_wide[:, PAIRS, :] + post_wide[:, PAIRS + 1, :]
    mass = jnp.broadcast_to(jnp.sum(totals, axis=0, keepdims=True), (LANES, LANES)).T[0:n_refs]
    scale = 1.0 / (mass[:, 0:1] + 1.0)
    first = pl.ds(a * img_dev, img_dev)
    mine = post_wide[first, PAIRS, :] + post_wide[first, PAIRS + 1, :]
    class_post[...] = jnp.concatenate([mine] * (LANES // img_dev), axis=0).T[n_refs : n_refs + CLASSES, 0:img_dev]
    weights = []
    for tp in range(PAIRS):
        both = post_wide[:, tp, :].T
        weights.append(jnp.concatenate([both[0:n_refs], both[n_refs : 2 * n_refs]], axis=1).astype(jnp.bfloat16))
    weights = jnp.concatenate(weights, axis=1)
    turned = rotated[...].reshape(SHIFTS * n_images, 2 * CHUNK)
    piece = lax.rem(r, per) * n_img + a

    target = r // per

    def out_copy(h, j):
        return exchange(
            out_send.at[h, j], out_buf.at[h, piece], out_ss.at[h, j], out_rs.at[h, piece], target, j
        )

    for h in range(CHUNK // STRIP):
        real = jnp.dot(weights, turned[:, h * STRIP : (h + 1) * STRIP], preferred_element_type=jnp.float32)
        imag = jnp.dot(
            weights, turned[:, CHUNK + h * STRIP : CHUNK + (h + 1) * STRIP], preferred_element_type=jnp.float32
        )
        real = (real * scale).reshape(n_ref, REF_ROWS, STRIP)
        imag = (imag * scale).reshape(n_ref, REF_ROWS, STRIP)
        out_send[h] = jnp.concatenate([real, imag], axis=1).astype(jnp.bfloat16)

        def out_start(i, carry):
            j = lax.rem(r + i, n_ref)
            here = (a == target) & (j == r)

            @pl.when(here)
            def _():
                out_buf[h, piece] = out_send[h, j]

            @pl.when(jnp.logical_not(here))
            def _():
                out_copy(h, j).start()

            return carry

        lax.fori_loop(0, n_ref, out_start, 0)

    for copy in img_copies + part_copies + own_copies:
        copy.wait_send()

    def post_sent(j, carry):
        post_copy(j).wait_send()
        return carry

    lax.fori_loop(1, n_dev, post_sent, 0)

    def ref_sent(j, carry):
        @pl.when(jnp.logical_not(ref_here(j)))
        def _():
            ref_copy(j).wait_send()

        return carry

    lax.fori_loop(0, n_ref, ref_sent, 0)
    for slot in range(per * CORES):
        stays, copy = ref_forward(slot)

        @pl.when(jnp.logical_not(stays))
        def _():
            copy.wait_send()

    for h in range(CHUNK // STRIP):
        for q in range(n_ref):
            @pl.when(jnp.logical_not(ref_here(q)))
            def _():
                exchange(
                    out_send.at[h, 0], out_buf.at[h, q], out_ss.at[h, 0], out_rs.at[h, q],
                    q % n_img, per * a + q // n_img,
                ).wait_recv()

            new_refs[:, q * CHUNK + h * STRIP : q * CHUNK + (h + 1) * STRIP] = out_buf[h, q]

    def out_sent(j, carry):
        @pl.when(jnp.logical_not((a == target) & (j == r)))
        def _():
            for h in range(CHUNK // STRIP):
                out_copy(h, j).wait_send()

        return carry

    lax.fori_loop(0, n_ref, out_sent, 0)


def widen_kernel(low, class_rows, new_refs, class_post):
    for q in range(low.shape[1] // CHUNK):
        px = slice(q * CHUNK, (q + 1) * CHUNK)
        block = low[:, px].astype(jnp.float32)
        new_refs[0, :, px] = block[0:REF_ROWS]
        new_refs[1, :, px] = block[REF_ROWS : 2 * REF_ROWS]
    class_post[...] = class_rows[...]


def fused(n_img, n_ref, images, references, precision, shifts, labels, log_prior):
    img_dev = images.shape[1]
    n_images = n_img * img_dev
    n_refs = n_ref * REF_ROWS
    n_dev = n_img * n_ref
    vmem = pl.BlockSpec(memory_space=pltpu.VMEM)
    far = pl.BlockSpec(memory_space=pl.ANY)
    low = jnp.bfloat16
    wide = jnp.float32
    strips = CHUNK // STRIP
    per = n_ref // n_img
    parts = (GROUPS, n_img)
    outs = (strips, n_ref)
    counts = ((6,), (n_img,), (n_img,), (n_ref,), (n_ref,), parts, parts)
    counts = counts + ((n_ref,), (n_ref,), (n_dev,), (n_dev,), outs, outs)
    counts = counts + ((CORES * per,), (CORES * per,))
    new_refs, class_rows = pl.pallas_call(
        functools.partial(fused_kernel, n_img, n_ref),
        out_shape=(
            jax.ShapeDtypeStruct((2 * REF_ROWS, references.shape[2]), low),
            jax.ShapeDtypeStruct((CLASSES, img_dev), wide),
        ),
        in_specs=[far] * 6,
        out_specs=(vmem, vmem),
        scratch_shapes=[
            pltpu.VMEM(images.shape, wide),
            pltpu.VMEM(references.shape, wide),
            pltpu.VMEM((1, img_dev), wide),
            pltpu.VMEM((2, SHIFTS), jnp.int32),
            pltpu.VMEM((1, REF_ROWS), jnp.int32),
            pltpu.VMEM((1, CLASSES), wide),
            pltpu.VMEM((n_img, 2, img_dev, CHUNK), low),
            pltpu.VMEM((n_img, 2, img_dev, CHUNK), low),
            pltpu.VMEM((n_ref, 2 * REF_ROWS, CHUNK), low),
            pltpu.VMEM((n_ref, 2 * REF_ROWS, CHUNK), low),
            pltpu.VMEM((SHIFTS, 8, CHUNK), wide),
            pltpu.VMEM((SHIFTS, 8, CHUNK), wide),
            pltpu.VMEM((SHIFTS, n_images, 2 * CHUNK), low),
            pltpu.VMEM((SHIFTS, n_refs, 2 * CHUNK), low),
            pltpu.VMEM((n_refs, LANES), wide),
            pltpu.VMEM((CORES * per, 2 * REF_ROWS, CHUNK), low),
            pltpu.VMEM((GROUPS, n_img, img_dev, TOGETHER * n_refs), wide),
            pltpu.VMEM((GROUPS, n_img - 1, img_dev, TOGETHER * n_refs), wide),
            pltpu.VMEM((img_dev, 8, LANES), wide),
            pltpu.VMEM((n_ref - 1, OWNED, 8, LANES), wide),
            pltpu.VMEM((n_dev, 16, LANES), low),
            pltpu.VMEM((n_images, 8, LANES), wide),
            pltpu.VMEM((strips, n_ref, 2 * REF_ROWS, STRIP), low),
            pltpu.VMEM((strips, n_ref, 2 * REF_ROWS, STRIP), low),
        ]
        + [pltpu.SemaphoreType.DMA(count) for count in counts],
        compiler_params=pltpu.CompilerParams(
            collective_id=0, has_side_effects=True, vmem_limit_bytes=56 * 1024 * 1024
        ),
        cost_estimate=pl.CostEstimate(flops=800_000_000, bytes_accessed=2_000_000, transcendentals=25_000),
    )(
        images,
        references,
        precision.reshape(1, img_dev),
        shifts.T,
        labels.reshape(1, REF_ROWS),
        log_prior.reshape(1, CLASSES),
    )
    new_refs, class_rows = pl.pallas_call(
        widen_kernel,
        out_shape=(
            jax.ShapeDtypeStruct(references.shape, wide),
            jax.ShapeDtypeStruct((CLASSES, img_dev), wide),
        ),
        in_specs=[vmem, vmem],
        out_specs=(vmem, vmem),
        cost_estimate=pl.CostEstimate(flops=0, bytes_accessed=800_000, transcendentals=0),
    )(new_refs, class_rows)
    return new_refs, class_rows.T


def local(n_img, n_ref, images, references, precision, shifts, labels, log_prior):
    fits = (
        images.shape[1] == OWNED * n_ref
        and images.shape[1] % 16 == 0
        and references.shape[1] == REF_ROWS
        and 2 * n_ref * REF_ROWS == LANES
        and images.shape[2] == n_img * CHUNK
        and references.shape[2] == n_ref * CHUNK
        and n_ref % n_img == 0
        and LANES % (n_img * images.shape[1]) == 0
        and n_img == 2 * CORES
    )
    if fits:
        return fused(n_img, n_ref, images, references, precision, shifts, labels, log_prior)
    return gathered(images, references, precision, shifts, labels, log_prior)


def solution(mesh):
    return jax.shard_map(
        functools.partial(local, mesh.shape["img"], mesh.shape["ref"]),
        mesh=mesh,
        in_specs=(P(None, "img", "ref"), P(None, "ref", "img"), P("img"), P(), P("ref"), P()),
        out_specs=(P(None, "ref", "img"), P("img", None)),
        check_vma=False,
    )
```

```python
import functools
import math

import jax
import jax.numpy as jnp
from jax import lax
from jax.experimental import pallas as pl
from jax.experimental.pallas import tpu as pltpu
from jax.sharding import PartitionSpec as P

ROWS = 256
COLS = 128
SHIFTS = 12
CLASSES = 4


def phases(shifts):
    index = jnp.arange(ROWS * COLS, dtype=jnp.int32)
    freq_y = (index // COLS - ROWS // 2).astype(jnp.float32)
    freq_x = (index % COLS).astype(jnp.float32)
    shift_x = shifts[:, 0].astype(jnp.float32)[:, None]
    shift_y = shifts[:, 1].astype(jnp.float32)[:, None]
    angles = 2.0 * math.pi / ROWS * (freq_x[None, :] * shift_x + freq_y[None, :] * shift_y)
    return (jnp.cos(angles), jnp.sin(angles))


def inner_rows(left, right):
    return lax.dot_general(
        left, right, (((1,), (1,)), ((), ())), preferred_element_type=jnp.float32
    )


def inner_cols(left, right):
    return lax.dot_general(
        left, right, (((0,), (0,)), ((), ())), preferred_element_type=jnp.float32
    )


def gathered(images, references, precision, shifts, labels, log_prior):
    img_low = lax.all_gather(images.astype(jnp.bfloat16), "ref", axis=2, tiled=True)
    ref_low = lax.all_gather(references.astype(jnp.bfloat16), "img", axis=2, tiled=True)
    pixels = img_low.shape[2]
    img_dev = img_low.shape[1]
    ref_dev = ref_low.shape[1]
    blocks = SHIFTS // 4
    cosine, sine_part = phases(shifts)
    cos_blocks = cosine.reshape(blocks, 4, pixels)
    sin_blocks = sine_part.reshape(blocks, 4, pixels)
    ref_wide = ref_low.astype(jnp.float32)
    energy = jnp.sum(ref_wide * ref_wide, axis=(0, 2))
    onehot = (labels[:, None] == jnp.arange(CLASSES, dtype=jnp.int32)[None, :]).astype(jnp.float32)
    prior_term = jnp.sum(onehot * log_prior[None, :], axis=1)

    def cross_block(operands):
        cos_rows, sin_rows = operands
        shifted_re = (
            ref_wide[0][None] * cos_rows[:, None, :] + ref_wide[1][None] * sin_rows[:, None, :]
        ).astype(jnp.bfloat16)
        shifted_im = (
            ref_wide[1][None] * cos_rows[:, None, :] - ref_wide[0][None] * sin_rows[:, None, :]
        ).astype(jnp.bfloat16)
        return inner_rows(img_low[0], shifted_re.reshape(4 * ref_dev, pixels)) + inner_rows(
            img_low[1], shifted_im.reshape(4 * ref_dev, pixels)
        )

    cross_terms = lax.map(cross_block, (cos_blocks, sin_blocks))
    cross_terms = jnp.transpose(cross_terms, (1, 0, 2)).reshape(img_dev, SHIFTS, ref_dev)
    scores = (
        precision[:, None, None] * (cross_terms - 0.5 * energy[None, None, :])
        + prior_term[None, None, :]
    )
    local_top = jnp.max(scores, axis=(1, 2))
    top_score = lax.pmax(local_top, "ref")
    exponent = jnp.exp(scores - top_score[:, None, None])
    local_class = jnp.einsum(
        "ik,kc->ic", jnp.sum(exponent, axis=1), onehot, precision=lax.Precision.HIGHEST
    )
    row_total, class_sum = lax.psum((jnp.sum(exponent, axis=(1, 2)), local_class), "ref")
    posterior = exponent / row_total[:, None, None]
    class_post = class_sum / row_total[:, None]
    local_mass = jnp.sum(posterior, axis=(0, 1))
    post_low = posterior.astype(jnp.bfloat16).reshape(img_dev, blocks, 4 * ref_dev)
    post_low = jnp.transpose(post_low, (1, 0, 2))

    def back_block(running, operands):
        weights_blk, cos_rows, sin_rows = operands
        back_re = inner_cols(weights_blk, img_low[0]).reshape(4, ref_dev, pixels)
        back_im = inner_cols(weights_blk, img_low[1]).reshape(4, ref_dev, pixels)
        part_re = jnp.sum(back_re * cos_rows[:, None, :] - back_im * sin_rows[:, None, :], axis=0)
        part_im = jnp.sum(back_im * cos_rows[:, None, :] + back_re * sin_rows[:, None, :], axis=0)
        return (running + jnp.stack([part_re, part_im]), None)

    start_sum = jnp.zeros((2, ref_dev, pixels), jnp.float32)
    summed, unused = lax.scan(back_block, start_sum, (post_low, cos_blocks, sin_blocks))
    summed_part = lax.psum_scatter(summed, "img", scatter_dimension=2, tiled=True)
    ref_mass = lax.psum(local_mass, "img")
    new_refs = summed_part / (ref_mass + 1.0)[None, :, None]
    return (new_refs, class_post)


MESH = pl.DeviceIdType.MESH
LANES = 128
CHUNK = 1024
OWNED = 2
PAIRS = SHIFTS // 2
TOGETHER = 4
GROUPS = SHIFTS // TOGETHER
STRIP = 512
CORES = 2
REF_ROWS = 8


def exchange(src, dst, send_sem, recv_sem, img, ref):
    return pltpu.make_async_remote_copy(
        src_ref=src, dst_ref=dst, send_sem=send_sem, recv_sem=recv_sem, device_id=(img, ref), device_id_type=MESH
    )


def fused_kernel(
    n_img, n_ref,
    images_hbm, references_hbm, precision_hbm, shifts_hbm, labels_hbm, log_prior_hbm,
    new_refs, class_post,
    images, references, precision, shifts, labels, log_prior,
    img_send, img_buf, ref_send, ref_buf, cos_tab, sin_tab, rotated, shifted,
    energy_col, ref_mid, part, part_in, own, own_in, post_buf, post_wide, out_send, out_buf, in_sem,
    img_ss, img_rs, ref_ss, ref_rs, part_ss, part_rs, own_ss, own_rs, post_ss, post_rs, out_ss, out_rs,
    ref_mid_ss, ref_mid_rs,
):
    n_dev = n_img * n_ref
    a = lax.axis_index("img")
    r = lax.axis_index("ref")
    me = a * n_ref + r
    per = n_ref // n_img
    img_dev = images.shape[1]
    n_images = n_img * img_dev
    n_refs = n_ref * REF_ROWS

    loads = [
        pltpu.make_async_copy(src, dst, in_sem.at[i])
        for i, (src, dst) in enumerate(
            (
                (references_hbm, references),
                (images_hbm, images),
                (shifts_hbm, shifts),
                (precision_hbm, precision),
                (labels_hbm, labels),
                (log_prior_hbm, log_prior),
            )
        )
    ]
    for load in loads:
        load.start()

    barrier = pltpu.get_barrier_semaphore()

    def greet(j, carry):
        other = lax.rem(me + j, n_dev)
        pl.semaphore_signal(barrier, inc=1, device_id=(other // n_ref, lax.rem(other, n_ref)), device_id_type=MESH)
        return carry

    lax.fori_loop(1, n_dev, greet, 0)

    loads[0].wait()
    for q in range(n_ref):
        px = pl.ds(q * CHUNK, CHUNK)
        both = jnp.concatenate([references[0, :, px], references[1, :, px]], axis=0)
        ref_send[q] = both.astype(jnp.bfloat16)

    pl.semaphore_wait(barrier, n_dev - 1)

    y, core = a // CORES, lax.rem(a, CORES)
    across = (1 - y) * CORES + core

    def ref_here(q):
        return (lax.rem(q, n_img) == a) & (per * a + q // n_img == r)

    def ref_by_way(q):
        at_mid = (lax.rem(q, n_img) == across) & (per * a + q // n_img == r)
        return (lax.rem(q, n_img) // CORES != y) & jnp.logical_not(at_mid)

    def ref_copy(q):
        return exchange(
            ref_send.at[q], ref_buf.at[r], ref_ss.at[q], ref_rs.at[r], lax.rem(q, n_img), per * a + q // n_img
        )

    def ref_hop(q):
        slot = (q // n_img) * CORES + lax.rem(q, CORES)
        return exchange(ref_send.at[q], ref_mid.at[slot], ref_ss.at[q], ref_mid_rs.at[slot], across, r)

    def hop_start(j, carry):
        q = lax.rem(me + j, n_ref)

        @pl.when(ref_by_way(q))
        def _():
            ref_hop(q).start()

        return carry

    lax.fori_loop(0, n_ref, hop_start, 0)

    def ref_start(j, carry):
        q = lax.rem(me + j, n_ref)
        here = ref_here(q)

        @pl.when(here)
        def _():
            ref_buf[r] = ref_send[q]

        @pl.when(jnp.logical_not(here | ref_by_way(q)))
        def _():
            ref_copy(q).start()

        return carry

    lax.fori_loop(0, n_ref, ref_start, 0)

    def ref_forward(slot):
        to_img = y * CORES + slot % CORES
        to_ref = per * across + slot // CORES
        return (to_img == a) & (to_ref == r), exchange(
            ref_mid.at[slot], ref_buf.at[r], ref_mid_ss.at[slot], ref_rs.at[r], to_img, to_ref
        )

    loads[1].wait()
    for q in range(n_img):
        img_send[q] = images[:, :, q * CHUNK : (q + 1) * CHUNK].astype(jnp.bfloat16)
    img_buf[a] = img_send[a]
    img_copies = []
    for j in range(1, n_img):
        dest = lax.rem(a + j, n_img)
        copy = exchange(img_send.at[dest], img_buf.at[a], img_ss.at[j], img_rs.at[j], dest, r)
        copy.start()
        img_copies.append(copy)

    for slot in range(per * CORES):
        stays, copy = ref_forward(slot)

        @pl.when(jnp.logical_not(stays))
        def _():
            exchange(ref_send.at[0], ref_mid.at[slot], ref_ss.at[0], ref_mid_rs.at[slot], across, r).wait_recv()
            copy.start()

    row_first = r * (n_img * CHUNK // COLS) + a * (CHUNK // COLS) - ROWS // 2
    freq_y = lax.broadcasted_iota(jnp.int32, (CHUNK // COLS, COLS), 0) + row_first
    freq_x = lax.broadcasted_iota(jnp.int32, (CHUNK // COLS, COLS), 1)

    for load in loads[2:]:
        load.wait()
    for t in range(SHIFTS):
        turn = freq_x * shifts[0:1, t : t + 1] + freq_y * shifts[1:2, t : t + 1]
        turn = ((turn + ROWS // 2) & (ROWS - 1)) - ROWS // 2
        angle = turn.astype(jnp.float32) * (2.0 * math.pi / ROWS)
        cosine = jnp.cos(angle)
        sine = jnp.sin(angle)
        for n in range(CHUNK // COLS):
            px = slice(n * COLS, (n + 1) * COLS)
            cos_tab[t, :, px] = jnp.broadcast_to(cosine[n : n + 1], (8, COLS))
            sin_tab[t, :, px] = jnp.broadcast_to(sine[n : n + 1], (8, COLS))

    row = lax.broadcasted_iota(jnp.int32, (8, LANES), 0)
    lane = lax.broadcasted_iota(jnp.int32, (8, LANES), 1)
    label_row = jnp.concatenate([labels[...].astype(jnp.float32)] * (LANES // REF_ROWS), axis=1)
    label_row = jnp.where((lane // REF_ROWS) % n_ref == r, jnp.broadcast_to(label_row, (8, LANES)), 0.0)

    def arrive(b):
        @pl.when(jnp.logical_not((a == r // per) & (b == r)))
        def _():
            exchange(ref_send.at[0], ref_buf.at[b], ref_ss.at[0], ref_rs.at[b], r // per, b).wait_recv()

    def shift(b, t):
        cos_row = cos_tab[t]
        sin_row = sin_tab[t]
        res = []
        ims = []
        for s in range(2):
            block = ref_buf[b + s].astype(jnp.float32)
            re = block[0:REF_ROWS]
            im = block[REF_ROWS : 2 * REF_ROWS]
            res.append(re * cos_row + im * sin_row)
            ims.append(im * cos_row - re * sin_row)
        rows = pl.ds(pl.multiple_of(b * REF_ROWS, 2 * REF_ROWS), 2 * REF_ROWS)
        shifted[t, rows, 0:CHUNK] = jnp.concatenate(res, axis=0).astype(jnp.bfloat16)
        shifted[t, rows, CHUNK : 2 * CHUNK] = jnp.concatenate(ims, axis=0).astype(jnp.bfloat16)

    def ready(b):
        arrive(b)
        arrive(b + 1)
        for s in range(2):
            block = ref_buf[b + s].astype(jnp.float32)
            square = jnp.sum(block * block, axis=1, keepdims=True)
            square = jnp.broadcast_to(square[0:REF_ROWS] + square[REF_ROWS : 2 * REF_ROWS], (REF_ROWS, LANES))
            energy_col[pl.ds(pl.multiple_of((b + s) * REF_ROWS, REF_ROWS), REF_ROWS)] = square

    layers = n_ref // 2

    def layer_step(i, carry):
        b = 2 * lax.rem(r // 2 + i, layers)
        ready(b)

        def turn_step(t, inner):
            shift(b, t)
            return inner

        return lax.fori_loop(0, SHIFTS, turn_step, carry)

    lax.fori_loop(0, layers - 1, layer_step, 0)
    last = 2 * lax.rem(r // 2 + layers - 1, layers)
    ready(last)
    energy = energy_col[...]
    half_energy = 0.5 * jnp.concatenate([energy, energy], axis=0).T[0:8][None]

    for copy in img_copies:
        copy.wait_recv()

    def rotate(t, carry):
        cos_row = cos_tab[t][None]
        sin_row = sin_tab[t][None]
        for b in range(n_img):
            re = img_buf[b, 0].astype(jnp.float32).reshape(img_dev // 8, 8, CHUNK)
            im = img_buf[b, 1].astype(jnp.float32).reshape(img_dev // 8, 8, CHUNK)
            rows = pl.ds(b * img_dev, img_dev)
            turned_re = (re * cos_row - im * sin_row).reshape(img_dev, CHUNK)
            turned_im = (im * cos_row + re * sin_row).reshape(img_dev, CHUNK)
            rotated[t, rows, 0:CHUNK] = turned_re.astype(jnp.bfloat16)
            rotated[t, rows, CHUNK : 2 * CHUNK] = turned_im.astype(jnp.bfloat16)
        return carry

    pictures = [img_buf[:, c].reshape(n_images, CHUNK) for c in range(2)]
    pictures = jnp.concatenate(pictures, axis=1)
    pictures = jnp.concatenate([pictures] * (LANES // n_images), axis=0)
    part_copies = []
    for g in range(GROUPS):
        for t in range(g * TOGETHER, (g + 1) * TOGETHER):
            shift(last, t)
        group = shifted[g * TOGETHER : (g + 1) * TOGETHER].reshape(TOGETHER * n_refs, 2 * CHUNK)
        cross = inner_rows(group, pictures).T[0:n_images]
        for h in range(TOGETHER // 2):
            pair = cross[:, h * LANES : (h + 1) * LANES]
            pair = (pair.reshape(n_images // 8, 8, LANES) - half_energy).reshape(n_img, img_dev, LANES)
            part[g, :, :, h * LANES : (h + 1) * LANES] = pair
        for j in range(1, n_img):
            dest = lax.rem(a + j, n_img)
            copy = exchange(
                part.at[g, dest], part_in.at[g, j - 1], part_ss.at[g, j], part_rs.at[g, j], dest, r
            )
            copy.start()
            part_copies.append(copy)

    own[...] = jnp.zeros_like(own)
    own[:, PAIRS, :] = jnp.broadcast_to(label_row[0:1], (img_dev, LANES))
    lax.fori_loop(0, TOGETHER, rotate, 0)
    for copy in part_copies:
        copy.wait_recv()
    for g in range(GROUPS):
        total = part[g, a]
        for j in range(n_img - 1):
            total = total + part_in[g, j]
        for h in range(TOGETHER // 2):
            own[:, g * (TOGETHER // 2) + h, :] = total[:, h * LANES : (h + 1) * LANES]
    own_copies = []
    for j in range(1, n_ref):
        dest = lax.rem(r + j, n_ref)
        copy = exchange(own.at[pl.ds(OWNED * dest, OWNED)], own_in.at[j - 1], own_ss.at[j], own_rs.at[j], a, dest)
        copy.start()
        own_copies.append(copy)
    lax.fori_loop(TOGETHER, 2 * TOGETHER, rotate, 0)
    for copy in own_copies:
        copy.wait_recv()
    mine = own[pl.ds(OWNED * r, OWNED)]
    for j in range(n_ref - 1):
        mine = mine + own_in[j]
    label_lane = jnp.broadcast_to(mine[0, PAIRS : PAIRS + 1], (8, LANES))
    prior = jnp.zeros((8, LANES), jnp.float32)
    for c in range(CLASSES):
        prior = prior + jnp.where(label_lane == c, log_prior[:, c : c + 1], 0.0)
    image_lane = lax.broadcasted_iota(jnp.int32, (1, img_dev), 1)

    blocks = []
    for il in range(OWNED):
        noise = jnp.sum(jnp.where(image_lane == OWNED * r + il, precision[...], 0.0), axis=1, keepdims=True)
        scores = noise * mine[il] + prior
        scores = jnp.where(row < PAIRS, scores, -jnp.inf)
        top = jnp.max(jnp.max(scores, axis=1, keepdims=True), axis=0, keepdims=True)
        exponent = jnp.exp(scores - top)
        row_total = jnp.sum(jnp.sum(exponent, axis=1, keepdims=True), axis=0, keepdims=True)
        posterior = exponent / row_total
        lane_sum = jnp.broadcast_to(jnp.sum(posterior, axis=0, keepdims=True), (8, LANES))
        totals = lane_sum + pltpu.roll(lane_sum, n_refs, 1)
        for c in range(CLASSES):
            in_class = jnp.sum(jnp.where(label_lane == c, lane_sum, 0.0), axis=1, keepdims=True)
            totals = jnp.where(lane == n_refs + c, in_class, totals)
        high = totals.astype(jnp.bfloat16).astype(jnp.float32)
        block = jnp.where(row == PAIRS, high, posterior)
        blocks.append(jnp.where(row == PAIRS + 1, totals - high, block))
    post_buf[me] = jnp.concatenate(blocks, axis=0).astype(jnp.bfloat16)

    post_copies = []
    for j in range(1, n_ref):
        dest = lax.rem(r + j, n_ref)
        copy = exchange(post_buf.at[me], post_buf.at[me], post_ss.at[j], post_rs.at[j], a, dest)
        copy.start()
        post_copies.append(copy)
    lax.fori_loop(2 * TOGETHER, SHIFTS, rotate, 0)
    for j in range(1, n_ref):
        source = lax.rem(r + n_ref - j, n_ref)
        exchange(
            post_buf.at[me], post_buf.at[a * n_ref + source], post_ss.at[j], post_rs.at[j], a, source
        ).wait_recv()
    group = pl.ds(a * n_ref, n_ref)
    for j in range(1, n_img):
        dest = lax.rem(a + j, n_img)
        k = n_ref + j
        copy = exchange(post_buf.at[group], post_buf.at[group], post_ss.at[k], post_rs.at[k], dest, r)
        copy.start()
        post_copies.append(copy)
    for j in range(1, n_img):
        source = lax.rem(a + n_img - j, n_img)
        k = n_ref + j
        theirs = post_buf.at[pl.ds(source * n_ref, n_ref)]
        exchange(post_buf.at[group], theirs, post_ss.at[k], post_rs.at[k], source, r).wait_recv()

    post_wide[...] = post_buf[...].astype(jnp.float32).reshape(n_images, 8, LANES)
    totals = post_wide[:, PAIRS, :] + post_wide[:, PAIRS + 1, :]
    mass = jnp.broadcast_to(jnp.sum(totals, axis=0, keepdims=True), (LANES, LANES)).T[0:n_refs]
    scale = 1.0 / (mass[:, 0:1] + 1.0)
    first = pl.ds(a * img_dev, img_dev)
    mine = post_wide[first, PAIRS, :] + post_wide[first, PAIRS + 1, :]
    class_post[...] = jnp.concatenate([mine] * (LANES // img_dev), axis=0).T[n_refs : n_refs + CLASSES, 0:img_dev]
    weights = []
    for tp in range(PAIRS):
        both = post_wide[:, tp, :].T
        weights.append(jnp.concatenate([both[0:n_refs], both[n_refs : 2 * n_refs]], axis=1).astype(jnp.bfloat16))
    weights = jnp.concatenate(weights, axis=1)
    turned = rotated[...].reshape(SHIFTS * n_images, 2 * CHUNK)
    piece = lax.rem(r, per) * n_img + a

    target = r // per

    def out_copy(h, j):
        return exchange(
            out_send.at[h, j], out_buf.at[h, piece], out_ss.at[h, j], out_rs.at[h, piece], target, j
        )

    for h in range(CHUNK // STRIP):
        real = jnp.dot(weights, turned[:, h * STRIP : (h + 1) * STRIP], preferred_element_type=jnp.float32)
        imag = jnp.dot(
            weights, turned[:, CHUNK + h * STRIP : CHUNK + (h + 1) * STRIP], preferred_element_type=jnp.float32
        )
        real = (real * scale).reshape(n_ref, REF_ROWS, STRIP)
        imag = (imag * scale).reshape(n_ref, REF_ROWS, STRIP)
        out_send[h] = jnp.concatenate([real, imag], axis=1).astype(jnp.bfloat16)

        def out_start(i, carry):
            j = lax.rem(r + i, n_ref)
            here = (a == target) & (j == r)

            @pl.when(here)
            def _():
                out_buf[h, piece] = out_send[h, j]

            @pl.when(jnp.logical_not(here))
            def _():
                out_copy(h, j).start()

            return carry

        lax.fori_loop(0, n_ref, out_start, 0)

    for copy in img_copies + part_copies + own_copies + post_copies:
        copy.wait_send()

    def ref_sent(j, carry):
        @pl.when(jnp.logical_not(ref_here(j)))
        def _():
            ref_copy(j).wait_send()

        return carry

    lax.fori_loop(0, n_ref, ref_sent, 0)
    for slot in range(per * CORES):
        stays, copy = ref_forward(slot)

        @pl.when(jnp.logical_not(stays))
        def _():
            copy.wait_send()

    for h in range(CHUNK // STRIP):
        for q in range(n_ref):
            @pl.when(jnp.logical_not(ref_here(q)))
            def _():
                exchange(
                    out_send.at[h, 0], out_buf.at[h, q], out_ss.at[h, 0], out_rs.at[h, q],
                    q % n_img, per * a + q // n_img,
                ).wait_recv()

            new_refs[:, q * CHUNK + h * STRIP : q * CHUNK + (h + 1) * STRIP] = out_buf[h, q]

    def out_sent(j, carry):
        @pl.when(jnp.logical_not((a == target) & (j == r)))
        def _():
            for h in range(CHUNK // STRIP):
                out_copy(h, j).wait_send()

        return carry

    lax.fori_loop(0, n_ref, out_sent, 0)


def widen_kernel(low, class_rows, new_refs, class_post):
    for q in range(low.shape[1] // CHUNK):
        px = slice(q * CHUNK, (q + 1) * CHUNK)
        block = low[:, px].astype(jnp.float32)
        new_refs[0, :, px] = block[0:REF_ROWS]
        new_refs[1, :, px] = block[REF_ROWS : 2 * REF_ROWS]
    class_post[...] = class_rows[...]


def fused(n_img, n_ref, images, references, precision, shifts, labels, log_prior):
    img_dev = images.shape[1]
    n_images = n_img * img_dev
    n_refs = n_ref * REF_ROWS
    n_dev = n_img * n_ref
    vmem = pl.BlockSpec(memory_space=pltpu.VMEM)
    far = pl.BlockSpec(memory_space=pl.ANY)
    low = jnp.bfloat16
    wide = jnp.float32
    strips = CHUNK // STRIP
    per = n_ref // n_img
    parts = (GROUPS, n_img)
    outs = (strips, n_ref)
    counts = ((6,), (n_img,), (n_img,), (n_ref,), (n_ref,), parts, parts)
    counts = counts + ((n_ref,), (n_ref,), (n_ref + n_img,), (n_ref + n_img,), outs, outs)
    counts = counts + ((CORES * per,), (CORES * per,))
    new_refs, class_rows = pl.pallas_call(
        functools.partial(fused_kernel, n_img, n_ref),
        out_shape=(
            jax.ShapeDtypeStruct((2 * REF_ROWS, references.shape[2]), low),
            jax.ShapeDtypeStruct((CLASSES, img_dev), wide),
        ),
        in_specs=[far] * 6,
        out_specs=(vmem, vmem),
        scratch_shapes=[
            pltpu.VMEM(images.shape, wide),
            pltpu.VMEM(references.shape, wide),
            pltpu.VMEM((1, img_dev), wide),
            pltpu.VMEM((2, SHIFTS), jnp.int32),
            pltpu.VMEM((1, REF_ROWS), jnp.int32),
            pltpu.VMEM((1, CLASSES), wide),
            pltpu.VMEM((n_img, 2, img_dev, CHUNK), low),
            pltpu.VMEM((n_img, 2, img_dev, CHUNK), low),
            pltpu.VMEM((n_ref, 2 * REF_ROWS, CHUNK), low),
            pltpu.VMEM((n_ref, 2 * REF_ROWS, CHUNK), low),
            pltpu.VMEM((SHIFTS, 8, CHUNK), wide),
            pltpu.VMEM((SHIFTS, 8, CHUNK), wide),
            pltpu.VMEM((SHIFTS, n_images, 2 * CHUNK), low),
            pltpu.VMEM((SHIFTS, n_refs, 2 * CHUNK), low),
            pltpu.VMEM((n_refs, LANES), wide),
            pltpu.VMEM((CORES * per, 2 * REF_ROWS, CHUNK), low),
            pltpu.VMEM((GROUPS, n_img, img_dev, TOGETHER * n_refs), wide),
            pltpu.VMEM((GROUPS, n_img - 1, img_dev, TOGETHER * n_refs), wide),
            pltpu.VMEM((img_dev, 8, LANES), wide),
            pltpu.VMEM((n_ref - 1, OWNED, 8, LANES), wide),
            pltpu.VMEM((n_dev, 16, LANES), low),
            pltpu.VMEM((n_images, 8, LANES), wide),
            pltpu.VMEM((strips, n_ref, 2 * REF_ROWS, STRIP), low),
            pltpu.VMEM((strips, n_ref, 2 * REF_ROWS, STRIP), low),
        ]
        + [pltpu.SemaphoreType.DMA(count) for count in counts],
        compiler_params=pltpu.CompilerParams(
            collective_id=0, has_side_effects=True, vmem_limit_bytes=56 * 1024 * 1024
        ),
        cost_estimate=pl.CostEstimate(flops=800_000_000, bytes_accessed=2_000_000, transcendentals=25_000),
    )(
        images,
        references,
        precision.reshape(1, img_dev),
        shifts.T,
        labels.reshape(1, REF_ROWS),
        log_prior.reshape(1, CLASSES),
    )
    new_refs, class_rows = pl.pallas_call(
        widen_kernel,
        out_shape=(
            jax.ShapeDtypeStruct(references.shape, wide),
            jax.ShapeDtypeStruct((CLASSES, img_dev), wide),
        ),
        in_specs=[vmem, vmem],
        out_specs=(vmem, vmem),
        cost_estimate=pl.CostEstimate(flops=0, bytes_accessed=800_000, transcendentals=0),
    )(new_refs, class_rows)
    return new_refs, class_rows.T


def local(n_img, n_ref, images, references, precision, shifts, labels, log_prior):
    fits = (
        images.shape[1] == OWNED * n_ref
        and images.shape[1] % 16 == 0
        and references.shape[1] == REF_ROWS
        and 2 * n_ref * REF_ROWS == LANES
        and images.shape[2] == n_img * CHUNK
        and references.shape[2] == n_ref * CHUNK
        and n_ref % n_img == 0
        and LANES % (n_img * images.shape[1]) == 0
        and n_img == 2 * CORES
    )
    if fits:
        return fused(n_img, n_ref, images, references, precision, shifts, labels, log_prior)
    return gathered(images, references, precision, shifts, labels, log_prior)


def solution(mesh):
    return jax.shard_map(
        functools.partial(local, mesh.shape["img"], mesh.shape["ref"]),
        mesh=mesh,
        in_specs=(P(None, "img", "ref"), P(None, "ref", "img"), P("img"), P(), P("ref"), P()),
        out_specs=(P(None, "ref", "img"), P("img", None)),
        check_vma=False,
    )
```
